256 devices in a mesh: fsdp: 16 (over z_lo, y), dp: 16 (over z_hi, x, core).
Axes of the slice: x: 4, y: 4, z: 8 (z_hi: 2, z_lo: 4; z = z_hi * 4 + z_lo), core: 2. Of those that a mesh axis runs over, the one named last changes fastest.
Arguments:
- block_in: bfloat16 [65536, 3072], P(('fsdp', 'dp')), may hold values from -6 to 6
- block_out: bfloat16 [65536, 3072], P(('fsdp', 'dp')), may hold values from -6 to 6
- weight: bfloat16 [3072, 3072], P('fsdp'), may hold values from -0.109375 to 0.109375
- adapter_a: bfloat16 [3072, 64], P('fsdp'), may hold values from -0.109375 to 0.109375
- adapter_b: bfloat16 [64, 3072], P(None, 'fsdp'), may hold values from -0.75 to 0.75
- proj: bfloat16 [3072, 64], replicated, may hold values from -0.109375 to 0.109375
- w_feature: bfloat16 [3136, 512], replicated, may hold values from -0.109375 to 0.109375
- w_embed: bfloat16 [512, 512], replicated, may hold values from -0.25 to 0.25
- id_table: bfloat16 [1024, 512], P('dp'), may hold values from -6 to 6
- box_rows: int32 [256, 6], P(('fsdp', 'dp')), may hold values from 0 to 9
- box_cols: int32 [256, 6], P(('fsdp', 'dp')), may hold values from 0 to 9
- identity: int32 [256, 6], P(('fsdp', 'dp')), may hold values from 0 to 1023, as said below
- face_count: int32 [256], P(('fsdp', 'dp')), may hold values from 3 to 6
Outputs:
- grad_in: bfloat16 [65536, 3072], P(('fsdp', 'dp'))
- grad_a: float32 [3072, 64], P('fsdp')
- grad_b: float32 [64, 3072], P(None, 'fsdp')
The draws below stay inside these ranges and needn't reach their ends.
Inputs may be any that keep to these rules, and one draw needn't show every extreme that they name: `identity`: identity blocks are runs of 64 numbers; at most 1 slots of an image name identities of one block.
All inputs are finite; a program needn't handle non-finite values.
Results may differ from the reference program's by a relative error of at most 0.03.
Values may be sent and summed in bfloat16 or wider, within the bound.
No kernel may reach another device: no remote copies, remote signals or barrier semaphores. Data moves between devices by JAX's collectives and lax.ppermute only.
A program may use at most 128 MiB of HBM per device.

```python
import jax
import jax.numpy as jnp
from jax import lax

D = 3072
CH = 64
RANK = 64
HID = 512
EMB = 512
FACE = 7
MAXF = 6
GW = 16
GH = 16
IDS_DEV = 64
CAP = 1
TOK_DEV = 256
CROP = 3136
SAMPLES = 256
TOKENS = 65536
IDS = 1024
N_DP = 16


def draw_identity(key, part):
    key = jax.random.fold_in(key, 11)
    keys = jax.random.split(key, 7)
    rotate = jax.random.randint(keys[0], (), 0, N_DP)
    lowest = jnp.minimum(jax.random.randint(keys[1], (SAMPLES,), 0, N_DP), jax.random.randint(keys[2], (SAMPLES,), 0, N_DP))
    lowest = jnp.minimum(lowest, jax.random.randint(keys[3], (SAMPLES,), 0, N_DP))
    base_block = (lowest + rotate) % N_DP
    scores = jax.random.randint(keys[5], (SAMPLES, MAXF), 0, 1000) * MAXF + jnp.arange(MAXF, dtype=jnp.int32)[None, :]
    pairing = jnp.argsort(scores, axis=1) // CAP
    blocks = (base_block[:, None] + pairing) % N_DP
    within = jax.random.randint(keys[6], (SAMPLES, MAXF), 0, IDS_DEV)
    return (blocks * IDS_DEV + within).astype(jnp.int32)


def draw_face_count(key, part):
    key = jax.random.fold_in(key, 23)
    keys = jax.random.split(key, 3)
    counts = 3 + jax.random.randint(keys[0], (SAMPLES,), 0, MAXF - 2)
    fullest = jax.random.randint(keys[2], (), 0, SAMPLES)
    return jnp.where(jnp.arange(SAMPLES) == fullest, MAXF, counts).astype(jnp.int32)


def with_ends(drawn, rng, smallest, top_value):
    longest = drawn.shape.index(max(drawn.shape))
    spots = []
    for shift in (0, 1):
        where = [jax.random.randint(jax.random.fold_in(rng, axis), (), 0, length) for axis, length in enumerate(drawn.shape)]
        where[longest] = (where[longest] + shift) % drawn.shape[longest]
        spots.append(tuple(where))
    return drawn.at[spots[0]].set(smallest).at[spots[1]].set(top_value)


def steps_of(key, dims, shards, least, largest):
    factor_of, own = 1.0, jax.random.fold_in(key, 6)
    for position, blocks in shards:
        draws = jnp.exp(jax.random.uniform(jax.random.fold_in(own, position), (blocks,), jnp.float32, least / len(shards), largest / len(shards)))
        factor_of = factor_of * jnp.repeat(draws, dims[position] // blocks).reshape([-1 if axis == position else 1 for axis in range(len(dims))])
    return factor_of


def noise(stream_key, shape, deviation, limit, shards=(), kind=jnp.bfloat16):
    factor_of = steps_of(stream_key, shape, shards, -0.22, 0.18) if shards else 1.0
    values = jax.random.normal(stream_key, shape, jnp.float32) * deviation * factor_of
    return jnp.minimum(jnp.maximum(values, -limit), limit).astype(kind)


def setup_inputs(seed: int = 0) -> dict:
    streams_of = jax.random.split(jax.random.key(seed), 14)
    return {
        "block_in": noise(streams_of[0], (TOKENS, D), 1.0, 6.0, ((0, 256),)),
        "block_out": noise(streams_of[1], (TOKENS, D), 1.0, 6.0, ((0, 256),)),
        "weight": noise(streams_of[2], (D, D), D ** -0.5, 0.109375, ((0, 16),)),
        "adapter_a": noise(streams_of[3], (D, RANK), D ** -0.5, 0.109375, ((0, 16),)),
        "adapter_b": noise(streams_of[4], (RANK, D), RANK ** -0.5, 0.75, ((1, 16),)),
        "proj": noise(streams_of[5], (D, CH), D ** -0.5, 0.109375),
        "w_feature": noise(streams_of[6], (CROP, HID), CROP ** -0.5, 0.109375),
        "w_embed": noise(streams_of[7], (HID, EMB), HID ** -0.5, 0.25),
        "id_table": noise(streams_of[8], (IDS, EMB), 1.0, 6.0, ((0, 16),)),
        "box_rows": with_ends(jax.random.randint(streams_of[9], (SAMPLES, MAXF), 0, GH - FACE + 1), jax.random.fold_in(streams_of[9], 1), 0, GH - FACE).astype(jnp.int32),
        "box_cols": with_ends(jax.random.randint(streams_of[10], (SAMPLES, MAXF), 0, GW - FACE + 1), jax.random.fold_in(streams_of[10], 1), 0, GW - FACE).astype(jnp.int32),
        "identity": draw_identity(jax.random.fold_in(streams_of[13], 71), 0),
        "face_count": draw_face_count(jax.random.fold_in(streams_of[13], 71), 0),
    }


loss_scale = 1024.0
eps_norm = 1e-06

def gelu_slope(preact):
    return jax.jvp(jax.nn.gelu, (preact,), (jnp.ones_like(preact),))[1]

def reward_grads(crops, refers, w_feature, w_embed):
    preact = jnp.dot(crops, w_feature, preferred_element_type=jnp.float32)
    feature = jax.nn.gelu(preact).astype(jnp.bfloat16)
    embedding = jnp.dot(feature, w_embed, preferred_element_type=jnp.float32)
    norm_e = jnp.sqrt(lax.optimization_barrier(jnp.sum(embedding * embedding, axis=-1, keepdims=True)) + eps_norm)
    norm_r = jnp.sqrt(lax.optimization_barrier(jnp.sum(refers * refers, axis=-1, keepdims=True)) + eps_norm)
    cosine = lax.optimization_barrier(jnp.sum(embedding * refers, axis=-1, keepdims=True)) / (norm_e * norm_r)
    d_embed = (loss_scale * (refers / (norm_e * norm_r) - cosine * embedding / (norm_e * norm_e))).astype(jnp.bfloat16)
    d_feature = lax.dot_general(d_embed, w_embed, (((1,), (1,)), ((), ())), preferred_element_type=jnp.float32)
    d_pre = (d_feature * gelu_slope(preact)).astype(jnp.bfloat16)
    return lax.dot_general(d_pre, w_feature, (((1,), (1,)), ((), ())), preferred_element_type=jnp.float32).astype(jnp.bfloat16)

def sample_grads(y_rows, row_start, col_start, ident, count, proj, id_table, w_feature, w_embed):
    latent = jnp.dot(y_rows, proj, preferred_element_type=jnp.float32).astype(jnp.bfloat16).reshape(GH, GW, CH)
    anchor = jnp.zeros((), jnp.int32)
    crops = jnp.stack([lax.dynamic_slice(latent, (row_start[number], col_start[number], anchor), (FACE, FACE, CH)).reshape(CROP) for number in range(MAXF)])
    alive = (jnp.arange(MAXF, dtype=jnp.int32) < count).astype(jnp.float32)[:, None]
    refers = id_table[ident].astype(jnp.float32) * alive
    d_crops = reward_grads(crops, refers, w_feature, w_embed)
    d_latent = jnp.zeros((GH, GW, CH), jnp.float32)
    for number in range(MAXF):
        corner = (row_start[number], col_start[number], anchor)
        window = lax.dynamic_slice(d_latent, corner, (FACE, FACE, CH))
        placed = d_crops[number].astype(jnp.float32).reshape(FACE, FACE, CH)
        d_latent = lax.dynamic_update_slice(d_latent, window + placed, corner)
    d_latent = d_latent.reshape(TOK_DEV, CH).astype(jnp.bfloat16)
    return lax.dot_general(d_latent, proj, (((1,), (1,)), ((), ())), preferred_element_type=jnp.float32).astype(jnp.bfloat16)

def reference(block_in, block_out, weight, adapter_a, adapter_b, proj, w_feature, w_embed, id_table, box_rows, box_cols, identity, face_count):

    def one_sample(carry, inputs):
        x_rows, y_rows, row_start, col_start, ident, count = inputs
        upstream = sample_grads(y_rows, row_start, col_start, ident, count, proj, id_table, w_feature, w_embed)
        low_grad = lax.dot_general(upstream, adapter_b, (((1,), (1,)), ((), ())), preferred_element_type=jnp.float32).astype(jnp.bfloat16)
        through = lax.dot_general(upstream, weight, (((1,), (1,)), ((), ())), preferred_element_type=jnp.float32)
        side = lax.dot_general(low_grad, adapter_a, (((1,), (1,)), ((), ())), preferred_element_type=jnp.float32)
        grad_rows = (upstream.astype(jnp.float32) + through + side).astype(jnp.bfloat16)
        x_low = jnp.dot(x_rows, adapter_a, preferred_element_type=jnp.float32).astype(jnp.bfloat16)
        term_a = lax.dot_general(x_rows, low_grad, (((0,), (0,)), ((), ())), preferred_element_type=jnp.float32)
        term_b = lax.dot_general(x_low, upstream, (((0,), (0,)), ((), ())), preferred_element_type=jnp.float32)
        return ((carry[0] + term_a, carry[1] + term_b), grad_rows)
    start_a = jnp.zeros((D, RANK), jnp.float32)
    start_b = jnp.zeros((RANK, D), jnp.float32)
    inputs = (block_in.reshape(SAMPLES, TOK_DEV, D), block_out.reshape(SAMPLES, TOK_DEV, D), box_rows, box_cols, identity, face_count)
    (sum_a, sum_b), grad_rows = lax.scan(one_sample, (start_a, start_b), inputs)
    return (grad_rows.reshape(TOKENS, D), sum_a / loss_scale, sum_b / loss_scale)
```

```python
import jax
import jax.numpy as jnp
from jax import lax
from jax.experimental import pallas as pl
from jax.experimental.pallas import tpu as pltpu
from jax.sharding import PartitionSpec as P

D = 3072
CH = 64
RANK = 64
HID = 512
EMB = 512
FACE = 7
MAXF = 6
GW = 16
IDS_DEV = 64
TOK = 256
CROP = 3136
SHARD = 192
HALF = 96
KH = 32
GROUPS = 12
ROWS = GROUPS * 8
SEGS = 12
PAY = HALF + KH

loss_scale = 1024.0
eps_norm = 1e-06
BF = jnp.bfloat16
F32 = jnp.float32
AXES = ("fsdp", "dp")


def coords(index):
    f, d = index // 16, index % 16
    return f // 4, f % 4, d // 8, (d // 2) % 4, d % 2


def number(zl, y, zh, x, c):
    return (zl * 4 + y) * 16 + zh * 8 + x * 2 + c


def pairs(move):
    return [(i, number(*move(*coords(i)))) for i in range(256)]


def shift_z(step):
    def move(zl, y, zh, x, c):
        z = (zh * 4 + zl + step) % 8
        return z % 4, y, z // 4, x, c

    return pairs(move)


CORE = pairs(lambda zl, y, zh, x, c: (zl, y, zh, x, c ^ 1))
X1 = pairs(lambda zl, y, zh, x, c: (zl, y, zh, x ^ 1, c))
X3 = pairs(lambda zl, y, zh, x, c: (zl, y, zh, x ^ 3, c))
Y1 = pairs(lambda zl, y, zh, x, c: (zl, y ^ 1, zh, x, c))
Y3 = pairs(lambda zl, y, zh, x, c: (zl, y ^ 3, zh, x, c))
ZL1 = pairs(lambda zl, y, zh, x, c: (zl ^ 1, y, zh, x, c))
ZL2 = pairs(lambda zl, y, zh, x, c: (zl ^ 2, y, zh, x, c))
ZPAIR = pairs(lambda zl, y, zh, x, c: (zl ^ 2, y, zh ^ 1, x, c))


def swap(value, perm):
    return lax.ppermute(value, AXES, perm)


def dot(a, b, da, db):
    return lax.dot_general(a, b, (((da,), (db,)), ((), ())), preferred_element_type=F32)


def lanes_at(width, offset):
    rows = lax.broadcasted_iota(jnp.int32, (CH, width), 0)
    cols = lax.broadcasted_iota(jnp.int32, (CH, width), 1)
    return (cols == rows + offset).astype(BF)


def params(mib):
    return pltpu.CompilerParams(vmem_limit_bytes=mib << 20)


def vmem(n):
    return [pl.BlockSpec(memory_space=pltpu.VMEM)] * n


SMEM = pl.BlockSpec(memory_space=pltpu.SMEM)


def pack_kernel(place, weight, proj, a_ref, b_ref, pay, own_proj):
    f, c = place[0], place[1]
    top = pl.multiple_of(c * HALF, 32)
    mine = proj[pl.ds(pl.multiple_of(f * SHARD, 64), SHARD), :]
    own_proj[...] = mine
    half = proj[pl.ds(pl.multiple_of(f * SHARD + c * HALF, 32), HALF), :]
    moved = dot(weight[pl.ds(top, HALF), :], proj[...], 1, 0) + half.astype(F32)
    left = dot(moved.astype(BF), lanes_at(128, 0), 1, 0)
    right = dot(a_ref[pl.ds(top, HALF), :], lanes_at(128, CH), 1, 0)
    pay[0:HALF, :] = (left + right).astype(BF)
    cross = dot(mine, b_ref[...], 0, 1).astype(BF)
    wide = dot(cross, lanes_at(128, CH), 1, 0)
    pay[HALF:PAY, :] = jnp.where(c == 0, wide[0:KH], wide[KH : 2 * KH]).astype(BF)


def pack(place, weight, proj, a, b):
    return pl.pallas_call(
        pack_kernel,
        out_shape=(
            jax.ShapeDtypeStruct((PAY, 128), BF),
            jax.ShapeDtypeStruct((SHARD, CH), BF),
        ),
        in_specs=[SMEM] + vmem(4),
        out_specs=tuple(vmem(2)),
        compiler_params=params(16),
        name="pack",
    )(place, weight, proj, a, b)


def corner_of(rows, cols, slot):
    corner = jnp.zeros_like(slot)
    for k in range(MAXF):
        corner = jnp.where(slot == k, rows[0, k] * GW + cols[0, k], corner)
    return corner


def token_of(rows, cols, index, i):
    slot = index & 7
    p = 4 * (index >> 3) + i
    down = (p * 37) >> 8
    token = corner_of(rows, cols, slot) + down * GW + (p - down * FACE)
    return jnp.where((slot < MAXF) & (p < FACE * FACE), token, -1)


def face_kernel(rows, cols, y_ref, proj, w_feature, w_embed, pre_ref, emb_ref):
    latent = dot(y_ref[...], proj[...], 1, 0).astype(BF)
    n = ROWS + 8
    index = lax.broadcasted_iota(jnp.int32, (n, TOK), 0)
    token = lax.broadcasted_iota(jnp.int32, (n, TOK), 1)
    crops = jnp.zeros((n, 256), F32)
    for i in range(4):
        pick = (token_of(rows, cols, index, i) == token).astype(BF)
        wide = dot(latent, lanes_at(256, CH * i), 1, 0).astype(BF)
        crops += dot(pick, wide, 1, 0)
    crops = crops.astype(BF)
    pre = dot(crops[ROWS:n, 0:CH], w_feature[GROUPS * 256 : CROP, :], 1, 0)
    for g in range(GROUPS):
        pre += dot(crops[8 * g : 8 * g + 8, :], w_feature[256 * g : 256 * g + 256, :], 1, 0)
    pre_ref[...] = pre
    feature = jax.nn.gelu(pre).astype(BF)
    emb_ref[...] = dot(feature, w_embed[...], 1, 0)


def face(rows, cols, y, proj, w_feature, w_embed):
    return pl.pallas_call(
        face_kernel,
        out_shape=(
            jax.ShapeDtypeStruct((8, HID), F32),
            jax.ShapeDtypeStruct((8, EMB), F32),
        ),
        in_specs=[SMEM, SMEM] + vmem(4),
        out_specs=tuple(vmem(2)),
        compiler_params=params(24),
        name="face",
    )(rows, cols, y, proj, w_feature, w_embed)


def low_kernel(place, x_ref, mine, other, maps, low, cross):
    f, c = place[0], place[1]
    zl, y = f >> 2, f & 3
    for i in range(16):
        b0, b1, b2, b3 = i & 1, (i >> 1) & 1, (i >> 2) & 1, i >> 3
        j = (zl ^ (2 * b0 + b1)) * 4 + (y ^ (3 * b3) ^ b2)
        for source, half in ((mine, c), (other, 1 - c)):
            start = pl.multiple_of(j * SHARD + half * HALF, 32)
            maps[pl.ds(start, HALF), :] = source[i, 0:HALF, :]
    for source, half in ((mine, c), (other, 1 - c)):
        total = jnp.zeros((KH, 128), F32)
        for i in range(16):
            total += source[i, HALF:PAY, :].astype(F32)
        cross[pl.ds(pl.multiple_of(half * KH, KH), KH), :] = total
    low[...] = dot(x_ref[...], maps[...], 1, 0).astype(BF)


def low_maps(place, x, mine, other):
    return pl.pallas_call(
        low_kernel,
        out_shape=(
            jax.ShapeDtypeStruct((D, 128), BF),
            jax.ShapeDtypeStruct((TOK, 128), BF),
            jax.ShapeDtypeStruct((2 * KH, 128), F32),
        ),
        in_specs=[SMEM] + vmem(3),
        out_specs=tuple(vmem(3)),
        compiler_params=params(24),
        name="low",
    )(place, x, mine, other)


def gelu_slope(preact):
    return jax.jvp(jax.nn.gelu, (preact,), (jnp.ones_like(preact),))[1]


def main_kernel(
    place, rows, cols, ident, count, near, far, pre_ref, emb_ref, w_embed, w_feature,
    x_ref, low, cross, out, wide_ref,
):
    d, c = place[2], place[1]
    slot = lax.broadcasted_iota(jnp.int32, (8, 16), 0)
    lane = lax.broadcasted_iota(jnp.int32, (8, 16), 1)
    refer = jnp.zeros((8, EMB), F32)
    for k in range(MAXF):
        who = ident[0, k]
        block = who >> 6
        flip = block ^ d
        b2 = (flip >> 2) & 1
        b1 = ((flip >> 1) & 1) ^ b2
        spot = (b2 * 4 + b1 * 2 + (flip >> 3)) * IDS_DEV + (who & 63)
        start = pl.multiple_of((spot >> 4) * 16, 16)
        chunk = jnp.where((flip & 1) == 0, near[pl.ds(start, 16), :], far[pl.ds(start, 16), :])
        live = (slot == k) & (lane == (spot & 15)) & (k < count[0])
        refer += dot(live.astype(BF), chunk, 1, 0)
    emb = emb_ref[...]
    norm_e = jnp.sqrt(jnp.sum(emb * emb, axis=-1, keepdims=True) + eps_norm)
    norm_r = jnp.sqrt(jnp.sum(refer * refer, axis=-1, keepdims=True) + eps_norm)
    cosine = jnp.sum(emb * refer, axis=-1, keepdims=True) / (norm_e * norm_r)
    d_embed = (
        loss_scale * (refer / (norm_e * norm_r) - cosine * emb / (norm_e * norm_e))
    ).astype(BF)
    d_feature = dot(d_embed, w_embed[...], 1, 1)
    d_pre = (d_feature * gelu_slope(pre_ref[...])).astype(BF)
    parts = [
        dot(d_pre, w_feature[256 * g : 256 * g + 256, :], 1, 1) for g in range(GROUPS)
    ]
    d_crop = jnp.concatenate(parts, axis=0).astype(BF)
    last = dot(d_pre, w_feature[GROUPS * 256 : CROP, :], 1, 1).astype(BF)
    index = lax.broadcasted_iota(jnp.int32, (TOK, ROWS), 1)
    token = lax.broadcasted_iota(jnp.int32, (TOK, ROWS), 0)
    tail = lax.broadcasted_iota(jnp.int32, (TOK, 8), 1) + ROWS
    pick = (token_of(rows, cols, tail, 0) == token[:, 0:8]).astype(BF)
    d_latent = dot(pick, last, 1, 0)
    for i in range(4):
        pick = (token_of(rows, cols, index, i) == token).astype(BF)
        piece = dot(d_crop, lanes_at(256, CH * i), 1, 1).astype(BF)
        d_latent += dot(pick, piece, 1, 0)
    d_latent = d_latent.astype(BF)
    for g in range(2):
        for z in range(4):
            first = 768 * z + 384 * g
            part = dot(d_latent, x_ref[:, first : first + 384], 0, 0).astype(BF)
            for h in range(2):
                for t in range(3):
                    out[h, SEGS * g + 3 * z + t] = part[
                        KH * h : KH * h + KH, 128 * t : 128 * t + 128
                    ]
    part = dot(d_latent, low[...], 0, 0).astype(BF)
    for h in range(2):
        out[h, 2 * SEGS] = part[KH * h : KH * h + KH, :]
    widen = (lanes_at(128, 0).astype(F32) + cross[...]).astype(BF)
    wide_ref[...] = dot(d_latent, widen, 1, 0).astype(BF)


def main(place, rows, cols, ident, count, *rest):
    return pl.pallas_call(
        main_kernel,
        out_shape=(
            jax.ShapeDtypeStruct((2, 2 * SEGS + 1, KH, 128), BF),
            jax.ShapeDtypeStruct((TOK, 128), BF),
        ),
        in_specs=[SMEM] * 5 + vmem(9),
        out_specs=tuple(vmem(2)),
        compiler_params=params(28),
        name="main",
    )(place, rows, cols, ident, count, *rest)


def through_kernel(wide, maps, out):
    out[...] = dot(wide[...], maps[...], 1, 1).astype(BF)


def through(wide, maps):
    cols = 768
    return pl.pallas_call(
        through_kernel,
        out_shape=jax.ShapeDtypeStruct((TOK, D), BF),
        grid=(D // cols,),
        in_specs=[
            pl.BlockSpec((TOK, 128), lambda i: (0, 0)),
            pl.BlockSpec((cols, 128), lambda i: (i, 0)),
        ],
        out_specs=pl.BlockSpec((TOK, cols), lambda i: (0, i)),
        compiler_params=params(16),
        name="through",
    )(wide, maps)


def last_kernel(place, mine, other, cross, own_proj, grad_a, grad_b, total, rows):
    f, c = place[0], place[1]
    for source, half in ((mine, c), (other, 1 - c)):
        for t in range(4):
            total[pl.ds(pl.multiple_of(half * KH, KH), KH), 128 * t : 128 * t + 128] = source[t]
    cross_t = dot(cross[...].astype(BF), lanes_at(128, CH), 1, 1).astype(BF)
    rows[...] = dot(total[:, 0:384], cross_t, 0, 0)
    start = pl.multiple_of((f & 1) * SHARD, 64)
    grad_a[...] = rows[pl.ds(start, SHARD), :] / loss_scale
    both = dot(total[:, 384:512], own_proj[...], 0, 1)
    grad_b[...] = both[RANK : 2 * RANK, :] / loss_scale


def last(place, mine, other, cross, own_proj):
    return pl.pallas_call(
        last_kernel,
        out_shape=(
            jax.ShapeDtypeStruct((SHARD, RANK), F32),
            jax.ShapeDtypeStruct((RANK, SHARD), F32),
        ),
        in_specs=[SMEM] + vmem(4),
        out_specs=tuple(vmem(2)),
        scratch_shapes=[pltpu.VMEM((2 * KH, 512), BF), pltpu.VMEM((384, CH), F32)],
        compiler_params=params(8),
        name="last",
    )(place, mine, other, cross, own_proj)


def add(*terms):
    return sum(t.astype(F32) for t in terms).astype(BF)


def reduce_all(sums, f, d):
    zl, y, c = f // 4, f % 4, d % 2
    group = y // 2
    pick = lambda v, i, n: lax.dynamic_slice_in_dim(v, i, n, axis=0)
    keep = pick(sums, c, 1)[0]
    v = add(keep, swap(pick(sums, 1 - c, 1)[0], CORE))
    tail = v[2 * SEGS :]
    side = lambda g: jnp.concatenate([pick(v, SEGS * g, SEGS), tail])
    v = add(side(group), swap(side(1 - group), Y3))
    up, down = swap(v, shift_z(-1)), swap(v, shift_z(1))
    three, two = add(v, up, down), add(v, up)
    chunk = lambda w, i: jnp.concatenate([pick(w, 3 * (i % 4), 3), w[SEGS:]])
    far_up = swap(chunk(three, zl + 1), shift_z(-3))
    far_down = swap(chunk(two, zl + 3), shift_z(3))
    v = add(chunk(three, zl), far_up, far_down)
    v = add(v, swap(v, Y1))
    v = add(v, swap(v, X1))
    v = add(v, swap(v, X3))
    return v, swap(v, CORE)


def local(
    block_in,
    block_out,
    weight,
    adapter_a,
    adapter_b,
    proj,
    w_feature,
    w_embed,
    id_table,
    box_rows,
    box_cols,
    identity,
    face_count,
):
    f, d = lax.axis_index("fsdp"), lax.axis_index("dp")
    place = jnp.stack([f, d % 2, d]).astype(jnp.int32)

    near = id_table
    for perm in (ZPAIR, X1, X3):
        near = jnp.concatenate([near, swap(near, perm)])
    far = swap(near, CORE)

    pay, own_proj = pack(place, weight, proj, adapter_a, adapter_b)
    mine = pay[None]
    for perm in (ZL2, ZL1, Y1, Y3):
        mine = jnp.concatenate([mine, swap(mine, perm)])
    other = swap(mine, CORE)

    pre, emb = face(box_rows, box_cols, block_out, proj, w_feature, w_embed)
    maps, low, cross = low_maps(place, block_in, mine, other)
    sums, wide = main(
        place, box_rows, box_cols, identity, face_count,
        near, far, pre, emb, w_embed, w_feature, block_in, low, cross,
    )
    total, total_far = reduce_all(sums, f, d)
    grad_in = through(wide, maps)
    grad_a, grad_b = last(place, total, total_far, cross, own_proj)
    return grad_in, grad_a, grad_b


def solution(mesh):
    return jax.shard_map(
        local,
        mesh=mesh,
        in_specs=(
            P(("fsdp", "dp"), None),
            P(("fsdp", "dp"), None),
            P("fsdp", None),
            P("fsdp", None),
            P(None, "fsdp"),
            P(),
            P(),
            P(),
            P("dp", None),
            P(("fsdp", "dp"), None),
            P(("fsdp", "dp"), None),
            P(("fsdp", "dp"), None),
            P(("fsdp", "dp")),
        ),
        out_specs=(P(("fsdp", "dp"), None), P("fsdp", None), P(None, "fsdp")),
        check_vma=False,
    )
```

```python
import jax
import jax.numpy as jnp
from jax import lax
from jax.experimental import pallas as pl
from jax.experimental.pallas import tpu as pltpu
from jax.sharding import PartitionSpec as P

D = 3072
CH = 64
RANK = 64
HID = 512
EMB = 512
FACE = 7
MAXF = 6
GW = 16
IDS_DEV = 64
TOK = 256
CROP = 3136
SHARD = 192
PAIR = 2 * SHARD
KH = 32
GROUPS = 12
ROWS = GROUPS * 8
UNITS = 48
BLOCK = 512

loss_scale = 1024.0
eps_norm = 1e-06
BF = jnp.bfloat16
F32 = jnp.float32
AXES = ("fsdp", "dp")


def coords(index):
    f, d = index // 16, index % 16
    return f // 4, f % 4, d // 8, (d // 2) % 4, d % 2


def number(zl, y, zh, x, c):
    return (zl * 4 + y) * 16 + zh * 8 + x * 2 + c


def flip(zl=0, y=0, zh=0, x=0, c=0):
    move = lambda l, b, h, a, e: (l ^ zl, b ^ y, h ^ zh, a ^ x, e ^ c)
    return [(i, number(*move(*coords(i)))) for i in range(256)]


def send(value, perm):
    return lax.ppermute(value, AXES, perm)


def after(value, *others):
    return lax.optimization_barrier((value,) + others)[0]


def dot(a, b, da, db):
    return lax.dot_general(a, b, (((da,), (db,)), ((), ())), preferred_element_type=F32)


def shifted(rows, width, offset):
    r = lax.broadcasted_iota(jnp.int32, (rows, width), 0)
    c = lax.broadcasted_iota(jnp.int32, (rows, width), 1)
    return (c == r + offset).astype(BF)


def params(mib):
    return pltpu.CompilerParams(vmem_limit_bytes=mib << 20)


def cost(us):
    return pl.CostEstimate(flops=us, bytes_accessed=us, transcendentals=0)


def vmem(n):
    return [pl.BlockSpec(memory_space=pltpu.VMEM)] * n


SMEM = pl.BlockSpec(memory_space=pltpu.SMEM)


HBM = pl.BlockSpec(memory_space=pl.ANY)


def load_all(pairs_of, sems):
    copies = [pltpu.make_async_copy(a, b, sems.at[n]) for n, (a, b) in enumerate(pairs_of)]
    for copy in copies:
        copy.start()
    return copies


def corner_of(rows, cols, slot):
    corner = jnp.zeros_like(slot)
    for k in range(MAXF):
        corner = jnp.where(slot == k, rows[0, k] * GW + cols[0, k], corner)
    return corner


def token_of(rows, cols, index, i):
    slot = index & 7
    p = 4 * (index >> 3) + i
    down = (p * 37) >> 8
    token = corner_of(rows, cols, slot) + down * GW + (p - down * FACE)
    return jnp.where((slot < MAXF) & (p < FACE * FACE), token, -1)


def load_all(moves, sems):
    copies = [pltpu.make_async_copy(a, b, sems.at[n]) for n, (a, b) in enumerate(moves)]
    for copy in copies:
        copy.start()
    return copies


def pack_kernel(
    place, proj_hbm, weight_hbm, a_hbm, b_hbm, pay, own_ref,
    proj_t, weight, a_ref, b_ref, sems,
):
    f, c = place[0], place[1]
    copies = load_all(
        (
            (proj_hbm, proj_t),
            (weight_hbm, weight),
            (a_hbm, a_ref),
            (b_hbm, b_ref),
        ),
        sems,
    )
    for copy in copies:
        copy.wait()
    window = proj_t[:, pl.ds(pl.multiple_of((f >> 1) * PAIR, 128), PAIR)]
    own = dot(window, shifted(SHARD, PAIR, (f & 1) * SHARD), 1, 1).astype(BF)
    own_ref[...] = own

    @pl.when(c == 0)
    def _():
        pay[0] = dot(a_ref[...], shifted(SHARD, 256, 0), 1, 0).astype(BF)

    @pl.when(c == 1)
    def _():
        moved = (dot(proj_t[...], weight[...], 1, 1) + own.astype(F32)).astype(BF)
        cross = dot(own, b_ref[...], 1, 1).astype(BF)
        wide = dot(moved, shifted(SHARD, 256, 0), 1, 0)
        pay[0] = (wide + dot(cross, shifted(CH, 256, SHARD), 1, 0)).astype(BF)


def pack(*args):
    return pl.pallas_call(
        pack_kernel,
        out_shape=(
            jax.ShapeDtypeStruct((1, CH, 256), BF),
            jax.ShapeDtypeStruct((CH, SHARD), BF),
        ),
        in_specs=[SMEM] + [HBM] * 4,
        out_specs=tuple(vmem(2)),
        scratch_shapes=[
            pltpu.VMEM((CH, D), BF),
            pltpu.VMEM((SHARD, D), BF),
            pltpu.VMEM((RANK, SHARD), BF),
            pltpu.VMEM((RANK, SHARD), BF),
            pltpu.SemaphoreType.DMA((4,)),
        ],
        compiler_params=params(52),
        cost_estimate=cost(2),
        name="pack",
    )(*args)


def face_kernel(
    rows, cols, y_hbm, proj_hbm, feature_hbm, embed_hbm, pre_ref, emb_ref,
    y_ref, proj_t, w_feature, w_embed, sems,
):
    copies = load_all(
        (
            (proj_hbm, proj_t),
            (y_hbm, y_ref),
            (feature_hbm, w_feature),
            (embed_hbm, w_embed),
        ),
        sems,
    )
    n = ROWS + 8
    index = lax.broadcasted_iota(jnp.int32, (n, TOK), 0)
    token = lax.broadcasted_iota(jnp.int32, (n, TOK), 1)
    picks = [(token_of(rows, cols, index, i) == token).astype(BF) for i in range(4)]
    copies[0].wait()
    copies[1].wait()
    latent = dot(y_ref[...], proj_t[...], 1, 1).astype(BF)
    crops = jnp.zeros((n, 256), F32)
    for i in range(4):
        wide = dot(latent, shifted(CH, 256, CH * i), 1, 0).astype(BF)
        crops += dot(picks[i], wide, 1, 0)
    crops = crops.astype(BF)
    copies[2].wait()
    pre = dot(crops[ROWS:n, 0:CH], w_feature[GROUPS * 256 : CROP, :], 1, 0)
    for g in range(GROUPS):
        pre += dot(crops[8 * g : 8 * g + 8, :], w_feature[256 * g : 256 * g + 256, :], 1, 0)
    pre_ref[...] = pre
    feature = jax.nn.gelu(pre).astype(BF)
    copies[3].wait()
    emb_ref[...] = dot(feature, w_embed[...], 1, 0)


def face(*args):
    return pl.pallas_call(
        face_kernel,
        out_shape=(
            jax.ShapeDtypeStruct((8, HID), F32),
            jax.ShapeDtypeStruct((8, EMB), F32),
        ),
        in_specs=[SMEM, SMEM] + [HBM] * 4,
        out_specs=tuple(vmem(2)),
        scratch_shapes=[
            pltpu.VMEM((TOK, D), BF),
            pltpu.VMEM((CH, D), BF),
            pltpu.VMEM((CROP, HID), BF),
            pltpu.VMEM((HID, EMB), BF),
            pltpu.SemaphoreType.DMA((4,)),
        ],
        compiler_params=params(52),
        cost_estimate=cost(4),
        name="face",
    )(*args)


def side_by_side(f, c, kind, near, far, near_2, far_2):
    zl, y = f >> 2, f & 3
    even = (y & 1) == 0
    lane = lax.broadcasted_iota(jnp.int32, (CH, 128), 1)
    for step, (a_ref, b_ref) in enumerate(((near, near_2), (far, far_2))):
        own_y = y ^ (3 * step)
        first = even if step == 0 else jnp.logical_not(even)
        for i in range(4):
            crossed = (i & 1) + (i >> 1) + step
            here = (c ^ (crossed & 1)) == kind
            a = jnp.where(here, a_ref[i], b_ref[i])
            b = jnp.where(here, b_ref[i + 4], a_ref[i + 4])
            left = jnp.where(first, a, b).astype(F32)
            right = jnp.where(first, b, a).astype(F32)
            turned = pltpu.roll(right[:, 0:128], 64, 1)
            tiles = (
                left[:, 0:128],
                jnp.where(lane < 64, left[:, 128:256], turned),
                jnp.where(lane < 64, turned, pltpu.roll(right[:, 128:256], 64, 1)),
            )
            p = (zl ^ (2 * (i & 1) + (i >> 1))) * 2 + (own_y >> 1)
            yield p, [t.astype(BF) for t in tiles], left[:, 128:256] + right[:, 128:256]


def low_kernel(place, x_ref, latent, near, far, near_2, far_2, maps, keep, give):
    f, c = place[0], place[1]
    total = jnp.zeros((TOK, RANK), F32)
    for p, tiles, _ in side_by_side(f, c, 0, near, far, near_2, far_2):
        for t in range(3):
            spot = pl.ds(pl.multiple_of(p * PAIR + 128 * t, 128), 128)
            maps[:, spot] = tiles[t]
        spot = pl.ds(pl.multiple_of(p * PAIR, 128), PAIR)
        total += dot(x_ref[:, spot], maps[:, spot], 1, 1)
    part = dot(latent[...], dot(total.astype(BF), shifted(RANK, 128, 0), 1, 0).astype(BF), 0, 0)
    lane = lax.broadcasted_iota(jnp.int32, (KH, 128), 1)
    unit = jnp.where(lane < 64, part[0:KH], pltpu.roll(part[KH : 2 * KH], 64, 1)).astype(BF)
    top, bottom = unit[0 : KH // 2], unit[KH // 2 : KH]
    keep[0] = jnp.where(c == 0, top, bottom)
    give[0] = jnp.where(c == 0, bottom, top)


def low_maps(*args):
    share = jax.ShapeDtypeStruct((1, KH // 2, 128), BF)
    return pl.pallas_call(
        low_kernel,
        out_shape=(jax.ShapeDtypeStruct((RANK, D), BF), share, share),
        in_specs=[SMEM] + vmem(6),
        out_specs=tuple(vmem(3)),
        compiler_params=params(16),
        cost_estimate=cost(2),
        name="low",
    )(*args)


def gelu_slope(preact):
    return jax.jvp(jax.nn.gelu, (preact,), (jnp.ones_like(preact),))[1]


def main_kernel(
    place, rows, cols, ident, count, near_0, near_1, far_0, far_1,
    pre_ref, emb_ref, w_embed, w_feature, x_ref, keep, give, latent_ref,
):
    c, d = place[1], place[2]
    slot = lax.broadcasted_iota(jnp.int32, (8, 16), 0)
    lane = lax.broadcasted_iota(jnp.int32, (8, 16), 1)
    refer = jnp.zeros((8, EMB), F32)
    for k in range(MAXF):
        who = ident[0, k]
        apart = (who >> 6) ^ d
        dz, dx = apart >> 3, (apart >> 1) & 3
        here = ((apart ^ dz ^ dx) & 1) == 0
        spot = ((dx ^ (dx >> 1)) & 1) * 128 + dz * IDS_DEV + (who & 63)
        at = pl.ds(pl.multiple_of((spot >> 4) * 16, 16), 16)
        near = jnp.where(dx < 2, near_0[at, :], near_1[at, :])
        far = jnp.where(dx < 2, far_0[at, :], far_1[at, :])
        live = (slot == k) & (lane == (spot & 15)) & (k < count[0])
        refer += dot(live.astype(BF), jnp.where(here, near, far), 1, 0)
    emb = emb_ref[...]
    norm_e = jnp.sqrt(jnp.sum(emb * emb, axis=-1, keepdims=True) + eps_norm)
    norm_r = jnp.sqrt(jnp.sum(refer * refer, axis=-1, keepdims=True) + eps_norm)
    cosine = jnp.sum(emb * refer, axis=-1, keepdims=True) / (norm_e * norm_r)
    d_embed = (
        loss_scale * (refer / (norm_e * norm_r) - cosine * emb / (norm_e * norm_e))
    ).astype(BF)
    d_feature = dot(d_embed, w_embed[...], 1, 1)
    d_pre = (d_feature * gelu_slope(pre_ref[...])).astype(BF)
    parts = [
        dot(d_pre, w_feature[256 * g : 256 * g + 256, :], 1, 1) for g in range(GROUPS)
    ]
    d_crop = jnp.concatenate(parts, axis=0).astype(BF)
    last = dot(d_pre, w_feature[GROUPS * 256 : CROP, :], 1, 1).astype(BF)
    index = lax.broadcasted_iota(jnp.int32, (TOK, ROWS), 1)
    token = lax.broadcasted_iota(jnp.int32, (TOK, ROWS), 0)
    tail = lax.broadcasted_iota(jnp.int32, (TOK, 8), 1) + ROWS
    pick = (token_of(rows, cols, tail, 0) == token[:, 0:8]).astype(BF)
    d_latent = dot(pick, last, 1, 0)
    for i in range(4):
        pick = (token_of(rows, cols, index, i) == token).astype(BF)
        piece = dot(d_crop, shifted(CH, 256, CH * i), 1, 1).astype(BF)
        d_latent += dot(pick, piece, 1, 0)
    d_latent = d_latent.astype(BF)
    latent_ref[...] = d_latent
    lane = lax.broadcasted_iota(jnp.int32, (KH, 128), 1)
    for p in range(8):
        part = dot(d_latent, x_ref[:, p * PAIR : p * PAIR + PAIR], 0, 0)
        for u in range(6):
            top = part[0:KH, 128 * (u // 2) : 128 * (u // 2) + 128]
            bottom = part[KH : 2 * KH, 128 * (u // 2) : 128 * (u // 2) + 128]
            if u % 2 == 0:
                unit = jnp.where(lane < 64, top, pltpu.roll(bottom, 64, 1))
            else:
                unit = jnp.where(lane < 64, pltpu.roll(top, 64, 1), bottom)
            j = 2 * p + u // 3
            share(c, unit.astype(BF), keep, give, 4 * (j % 4) + j // 4, u % 3)


def share(c, unit, keep, give, j, u):
    top, bottom = unit[0 : KH // 2], unit[KH // 2 : KH]
    keep[j, u] = jnp.where(c == 0, top, bottom)
    give[j, u] = jnp.where(c == 0, bottom, top)


def main(*args):
    shares = jax.ShapeDtypeStruct((16, 3, KH // 2, 128), BF)
    return pl.pallas_call(
        main_kernel,
        out_shape=(shares, shares, jax.ShapeDtypeStruct((TOK, CH), BF)),
        in_specs=[SMEM] * 5 + vmem(9),
        out_specs=tuple(vmem(3)),
        compiler_params=params(24),
        cost_estimate=cost(3),
        name="main",
    )(*args)


def through_kernel(
    place, near, far, near_2, far_2, latent, maps, out, cross_ref, stack, slab, sems
):
    f, c = place[0], place[1]
    total = jnp.zeros((CH, 128), F32)
    for p, tiles, beside in side_by_side(f, c, 1, near, far, near_2, far_2):
        total += beside
        for t in range(3):
            stack[0:CH, pl.ds(pl.multiple_of(p * PAIR + 128 * t, 128), 128)] = tiles[t]
    cross_ref[...] = dot(total.astype(BF), shifted(CH, 128, 64), 1, 1).astype(BF)
    stack[CH : CH + RANK, :] = maps[...]
    widen = shifted(CH, 128, 0).astype(F32) + dot(cross_ref[...], shifted(RANK, 128, CH), 1, 0)
    wide = dot(latent[...], widen.astype(BF), 1, 0).astype(BF)
    copies = []
    for i in range(D // BLOCK):
        slab[i] = dot(wide, stack[:, BLOCK * i : BLOCK * i + BLOCK], 1, 0).astype(BF)
        copy = pltpu.make_async_copy(
            slab.at[i], out.at[:, pl.ds(BLOCK * i, BLOCK)], sems.at[i]
        )
        copy.start()
        copies.append(copy)
    for copy in copies:
        copy.wait()


def through(*args):
    return pl.pallas_call(
        through_kernel,
        out_shape=(
            jax.ShapeDtypeStruct((TOK, D), BF),
            jax.ShapeDtypeStruct((CH, RANK), BF),
        ),
        in_specs=[SMEM] + vmem(6),
        out_specs=(pl.BlockSpec(memory_space=pl.ANY), pl.BlockSpec(memory_space=pltpu.VMEM)),
        scratch_shapes=[
            pltpu.VMEM((CH + RANK, D), BF),
            pltpu.VMEM((D // BLOCK, TOK, BLOCK), BF),
            pltpu.SemaphoreType.DMA((D // BLOCK,)),
        ],
        compiler_params=params(16),
        cost_estimate=cost(3),
        name="through",
    )(*args)


def last_kernel(units, cross, own_proj, grad_a, grad_b):
    unit = [units[u] for u in range(4)]

    def rows(right):
        total = jnp.zeros((KH, SHARD), F32)
        for u in range(3):
            r = lax.broadcasted_iota(jnp.int32, (128, SHARD), 0) - 64 * right
            col = lax.broadcasted_iota(jnp.int32, (128, SHARD), 1) - 64 * u
            place_at = ((r == col) & (col >= 0) & (col < 64)).astype(BF)
            total += dot(unit[u], place_at, 1, 0)
        return total

    sums = jnp.concatenate([rows(0), rows(1)], axis=0).astype(BF)
    low = jnp.concatenate(
        [dot(unit[3], shifted(RANK, 128, 64 * h), 1, 1) for h in range(2)], axis=0
    ).astype(BF)
    grad_a[...] = dot(cross[...], sums, 0, 0) / loss_scale
    grad_b[...] = dot(low, own_proj[...], 0, 0) / loss_scale


def last(*args):
    return pl.pallas_call(
        last_kernel,
        out_shape=(
            jax.ShapeDtypeStruct((RANK, SHARD), F32),
            jax.ShapeDtypeStruct((RANK, SHARD), F32),
        ),
        in_specs=vmem(3),
        out_specs=tuple(vmem(2)),
        compiler_params=params(8),
        cost_estimate=cost(1),
        name="last",
    )(*args)


def add(*terms):
    return sum(t.astype(F32) for t in terms).astype(BF)


def widen(near, perm):
    return jnp.concatenate([near, send(near, perm)])


def exchange(v, groups):
    v = lax.all_to_all(v, AXES, 0, 0, axis_index_groups=groups, tiled=True)
    return jnp.sum(v.astype(F32), axis=0).astype(BF)


def beside(v, low):
    return jnp.concatenate([v, jnp.broadcast_to(low[None], v.shape[:1] + low.shape)], axis=1)


def shift_z(step):
    def move(zl, y, zh, x, c):
        z = (zh * 4 + zl + step) % 8
        return z % 4, y, z // 4, x, c

    return [(i, number(*move(*coords(i)))) for i in range(256)]


def slab_of(value, start, size):
    return lax.dynamic_slice_in_dim(value, start, size, axis=0)


def members(key):
    groups = {}
    for i in range(256):
        groups.setdefault(key(*coords(i)), []).append(i)
    return list(groups.values())


def reduce_all(keep, give, keep_low, give_low, f, c):
    zl, y = f // 4, f % 4
    v = add(keep, send(give, flip(c=1)))
    low = add(keep_low, send(give_low, flip(c=1)))
    v = beside(v.reshape((4, 12) + v.shape[2:]), low)
    v = exchange(v, members(lambda zl, y, zh, x, c: (zl, zh, x, c)))
    v, low = v[:12].reshape((4, 3) + v.shape[1:]), v[12:]
    v = beside(v, low)
    v = jnp.broadcast_to(v[:, None], (4, 2) + v.shape[1:]).reshape((8,) + v.shape[1:])
    v = exchange(v, members(lambda zl, y, zh, x, c: (y, x, c)))
    other = send(v, flip(c=1))
    v = jnp.concatenate([jnp.where(c == 0, v, other), jnp.where(c == 0, other, v)], axis=1)
    v = add(v, send(v, flip(x=1, c=1)))
    return add(v, send(v, flip(x=3, c=1)))


def local(
    block_in,
    block_out,
    weight,
    adapter_a,
    adapter_b,
    proj,
    w_feature,
    w_embed,
    id_table,
    box_rows,
    box_cols,
    identity,
    face_count,
):
    f, d = lax.axis_index("fsdp"), lax.axis_index("dp")
    place = jnp.stack([f, d % 2, d]).astype(jnp.int32)
    proj_t = proj.T

    table = widen(id_table, flip(zl=2, zh=1, c=1))
    maps, own_proj = pack(place, proj_t, weight, adapter_a.T, adapter_b)
    maps = widen(maps, flip(zl=2, c=1))
    table = widen(table, flip(x=1, c=1))
    maps = widen(maps, flip(zl=1, c=1))
    maps = widen(maps, flip(y=1, c=1))
    table = after(table, maps)
    pre, emb = face(
        after(box_rows, table, maps), box_cols, block_out, proj_t, w_feature, w_embed
    )
    table_2 = after(send(table, flip(x=3, c=1)), pre)
    maps_2 = after(send(maps, flip(y=3, c=1)), pre)
    table_far = (send(table, flip(c=1)), send(table_2, flip(c=1)))
    blocks = (maps, maps_2, send(maps, flip(c=1)), send(maps_2, flip(c=1)))
    keep, give, d_latent = main(
        place, box_rows, box_cols, identity, face_count,
        table, table_2, *table_far, pre, emb, w_embed, w_feature, block_in,
    )
    whole_a, keep_low, give_low = low_maps(place, block_in, d_latent, *blocks)
    total = reduce_all(keep, give, keep_low, give_low, f, d % 2)
    grad_in, cross = through(place, *blocks, d_latent, whole_a)
    grad_a, grad_b = last(total, cross, own_proj)
    return grad_in, grad_a.T, grad_b


def solution(mesh):
    return jax.shard_map(
        local,
        mesh=mesh,
        in_specs=(
            P(("fsdp", "dp"), None),
            P(("fsdp", "dp"), None),
            P("fsdp", None),
            P("fsdp", None),
            P(None, "fsdp"),
            P(),
            P(),
            P(),
            P("dp", None),
            P(("fsdp", "dp"), None),
            P(("fsdp", "dp"), None),
            P(("fsdp", "dp"), None),
            P(("fsdp", "dp")),
        ),
        out_specs=(P(("fsdp", "dp"), None), P("fsdp", None), P(None, "fsdp")),
        check_vma=False,
    )
```

```python
import jax
import jax.numpy as jnp
from jax import lax
from jax.experimental import pallas as pl
from jax.experimental.pallas import tpu as pltpu
from jax.sharding import PartitionSpec as P

D = 3072
CH = 64
RANK = 64
HID = 512
EMB = 512
FACE = 7
MAXF = 6
GW = 16
IDS_DEV = 64
TOK = 256
CROP = 3136
SHARD = 192
PAIR = 2 * SHARD
KH = 32
GROUPS = 12
ROWS = GROUPS * 8
UNITS = 48
BLOCK = 512

loss_scale = 1024.0
eps_norm = 1e-06
BF = jnp.bfloat16
F32 = jnp.float32
AXES = ("fsdp", "dp")


def coords(index):
    f, d = index // 16, index % 16
    return f // 4, f % 4, d // 8, (d // 2) % 4, d % 2


def number(zl, y, zh, x, c):
    return (zl * 4 + y) * 16 + zh * 8 + x * 2 + c


def flip(zl=0, y=0, zh=0, x=0, c=0):
    move = lambda l, b, h, a, e: (l ^ zl, b ^ y, h ^ zh, a ^ x, e ^ c)
    return [(i, number(*move(*coords(i)))) for i in range(256)]


def send(value, perm):
    return lax.ppermute(value, AXES, perm)


def after(value, *others):
    return lax.optimization_barrier((value,) + others)[0]


def dot(a, b, da, db):
    return lax.dot_general(a, b, (((da,), (db,)), ((), ())), preferred_element_type=F32)


def shifted(rows, width, offset):
    r = lax.broadcasted_iota(jnp.int32, (rows, width), 0)
    c = lax.broadcasted_iota(jnp.int32, (rows, width), 1)
    return (c == r + offset).astype(BF)


def params(mib):
    return pltpu.CompilerParams(vmem_limit_bytes=mib << 20)


def cost(us):
    return pl.CostEstimate(flops=us, bytes_accessed=us, transcendentals=0)


def vmem(n):
    return [pl.BlockSpec(memory_space=pltpu.VMEM)] * n


SMEM = pl.BlockSpec(memory_space=pltpu.SMEM)


HBM = pl.BlockSpec(memory_space=pl.ANY)


def corner_of(rows, cols, slot):
    corner = jnp.zeros_like(slot)
    for k in range(MAXF):
        corner = jnp.where(slot == k, rows[0, k] * GW + cols[0, k], corner)
    return corner


def token_of(rows, cols, index, i):
    slot = index & 7
    p = 4 * (index >> 3) + i
    down = (p * 37) >> 8
    token = corner_of(rows, cols, slot) + down * GW + (p - down * FACE)
    return jnp.where((slot < MAXF) & (p < FACE * FACE), token, -1)


def load_all(moves, sems):
    waits, n = [], 0
    for source, target, parts in moves:
        rows = source.shape[0] // parts
        copies = []
        for p in range(parts):
            at = pl.ds(p * rows, rows)
            copies.append(pltpu.make_async_copy(source.at[at], target.at[at], sems.at[n]))
            copies[-1].start()
            n += 1
        waits.append(copies)
    return waits


def arrived(*groups):
    for copies in groups:
        for copy in copies:
            copy.wait()


def front_kernel(
    rows, cols, proj_hbm, weight_hbm, a_hbm, b_hbm, y_hbm, feature_hbm, embed_hbm,
    pay, own_ref, face_ref,
    proj_t, weight, a_ref, b_ref, y_ref, w_feature, w_embed, sems,
):
    f, c = lax.axis_index("fsdp"), lax.axis_index("dp") & 1
    small, heavy, faces, feature_w, embed_w = (slice(0, 3), slice(3, 4), 4, 5, 6)
    copies = load_all(
        (
            (proj_hbm, proj_t, 2),
            (a_hbm, a_ref, 1),
            (b_hbm, b_ref, 1),
            (weight_hbm, weight, 4),
            (y_hbm, y_ref, 4),
            (feature_hbm, w_feature, 7),
            (embed_hbm, w_embed, 2),
        ),
        sems,
    )
    n = ROWS + 8
    index = lax.broadcasted_iota(jnp.int32, (n, TOK), 0)
    token = lax.broadcasted_iota(jnp.int32, (n, TOK), 1)
    picks = [(token_of(rows, cols, index, i) == token).astype(BF) for i in range(4)]
    arrived(*copies[small])
    window = proj_t[:, pl.ds(pl.multiple_of((f >> 1) * PAIR, 128), PAIR)]
    own = dot(window, shifted(SHARD, PAIR, (f & 1) * SHARD), 1, 1).astype(BF)
    own_ref[...] = own
    arrived(*copies[heavy])

    @pl.when(c == 0)
    def _():
        pay[0] = dot(a_ref[...], shifted(SHARD, 256, 0), 1, 0).astype(BF)

    @pl.when(c == 1)
    def _():
        moved = (dot(proj_t[...], weight[...], 1, 1) + own.astype(F32)).astype(BF)
        cross = dot(own, b_ref[...], 1, 1).astype(BF)
        wide = dot(moved, shifted(SHARD, 256, 0), 1, 0)
        pay[0] = (wide + dot(cross, shifted(CH, 256, SHARD), 1, 0)).astype(BF)

    arrived(copies[faces])
    latent = dot(y_ref[...], proj_t[...], 1, 1).astype(BF)
    crops = jnp.zeros((n, 256), F32)
    for i in range(4):
        wide = dot(latent, shifted(CH, 256, CH * i), 1, 0).astype(BF)
        crops += dot(picks[i], wide, 1, 0)
    crops = crops.astype(BF)
    arrived(copies[feature_w])
    pre = dot(crops[ROWS:n, 0:CH], w_feature[GROUPS * 256 : CROP, :], 1, 0)
    for g in range(GROUPS):
        pre += dot(crops[8 * g : 8 * g + 8, :], w_feature[256 * g : 256 * g + 256, :], 1, 0)
    face_ref[0:8] = pre
    feature = jax.nn.gelu(pre).astype(BF)
    arrived(copies[embed_w])
    face_ref[8:16] = dot(feature, w_embed[...], 1, 0)


def front(*args):
    return pl.pallas_call(
        front_kernel,
        out_shape=(
            jax.ShapeDtypeStruct((1, CH, 256), BF),
            jax.ShapeDtypeStruct((CH, SHARD), BF),
            jax.ShapeDtypeStruct((16, EMB), F32),
        ),
        in_specs=[SMEM] * 2 + [HBM] * 7,
        out_specs=tuple(vmem(3)),
        scratch_shapes=[
            pltpu.VMEM((CH, D), BF),
            pltpu.VMEM((SHARD, D), BF),
            pltpu.VMEM((RANK, SHARD), BF),
            pltpu.VMEM((RANK, SHARD), BF),
            pltpu.VMEM((TOK, D), BF),
            pltpu.VMEM((CROP, HID), BF),
            pltpu.VMEM((HID, EMB), BF),
            pltpu.SemaphoreType.DMA((21,)),
        ],
        compiler_params=params(56),
        cost_estimate=cost(4),
        name="front",
    )(*args)


def side_by_side(f, c, kind, maps):
    zl, y = f >> 2, f & 3
    even = (y & 1) == 0
    lane = lax.broadcasted_iota(jnp.int32, (CH, 128), 1)

    def block(k, i):
        crossed = int(k != 0) ^ int(i != 0)
        return jnp.where((c ^ crossed) == kind, maps[k][i], maps[k + 4][i])

    for k in (0, 2):
        for i in range(4):
            a, b = block(k, i), block(k + 1, i)
            left = jnp.where(even, a, b).astype(F32)
            right = jnp.where(even, b, a).astype(F32)
            turned = pltpu.roll(right[:, 0:128], 64, 1)
            tiles = (
                left[:, 0:128],
                jnp.where(lane < 64, left[:, 128:256], turned),
                jnp.where(lane < 64, turned, pltpu.roll(right[:, 128:256], 64, 1)),
            )
            p = (zl ^ i) * 2 + ((y ^ k) >> 1)
            yield p, [t.astype(BF) for t in tiles], left[:, 128:256] + right[:, 128:256]


def low_kernel(x_ref, latent, *refs):
    blocks, (maps, keep, give) = refs[0:8], refs[8:]
    f, c = lax.axis_index("fsdp"), lax.axis_index("dp") & 1
    total = jnp.zeros((TOK, RANK), F32)
    for p, tiles, _ in side_by_side(f, c, 0, blocks):
        for t in range(3):
            spot = pl.ds(pl.multiple_of(p * PAIR + 128 * t, 128), 128)
            maps[:, spot] = tiles[t]
        spot = pl.ds(pl.multiple_of(p * PAIR, 128), PAIR)
        total += dot(x_ref[:, spot], maps[:, spot], 1, 1)
    part = dot(latent[...], dot(total.astype(BF), shifted(RANK, 128, 0), 1, 0).astype(BF), 0, 0)
    lane = lax.broadcasted_iota(jnp.int32, (KH, 128), 1)
    unit = jnp.where(lane < 64, part[0:KH], pltpu.roll(part[KH : 2 * KH], 64, 1)).astype(BF)
    top, bottom = unit[0 : KH // 2], unit[KH // 2 : KH]
    half = parity(f, lax.axis_index("dp"))
    keep[0] = jnp.where(half == 0, top, bottom)
    give[0] = jnp.where(half == 0, bottom, top)


def low_maps(*args):
    share = jax.ShapeDtypeStruct((1, KH // 2, 128), BF)
    return pl.pallas_call(
        low_kernel,
        out_shape=(jax.ShapeDtypeStruct((RANK, D), BF), share, share),
        in_specs=vmem(10),
        out_specs=tuple(vmem(3)),
        compiler_params=params(16),
        cost_estimate=cost(2),
        name="low",
    )(*args)


def gelu_slope(preact):
    return jax.jvp(jax.nn.gelu, (preact,), (jnp.ones_like(preact),))[1]


def main_kernel(
    rows, cols, ident, count, *refs,
):
    near, far = refs[0:4], refs[4:8]
    face_ref, w_embed, w_feature, x_ref, keep, give, latent_ref = refs[8:]
    d = lax.axis_index("dp")
    half = parity(lax.axis_index("fsdp"), d)
    slot = lax.broadcasted_iota(jnp.int32, (8, 16), 0)
    lane = lax.broadcasted_iota(jnp.int32, (8, 16), 1)
    refer = jnp.zeros((8, EMB), F32)
    for k_slot in range(MAXF):
        who = ident[0, k_slot]
        apart = (who >> 6) ^ d
        dz, dx = apart >> 3, (apart >> 1) & 3
        crossed = dz ^ jnp.where(dx == 0, 0, 1)
        here = ((apart ^ crossed) & 1) == 0
        spot = dz * IDS_DEV + (who & 63)
        at = pl.ds(pl.multiple_of((spot >> 4) * 16, 16), 16)
        found = jnp.zeros((16, EMB), BF)
        for k in range(4):
            found = jnp.where(dx == k, jnp.where(here, near[k][at, :], far[k][at, :]), found)
        live = (slot == k_slot) & (lane == (spot & 15)) & (k_slot < count[0])
        refer += dot(live.astype(BF), found, 1, 0)
    emb = face_ref[8:16]
    norm_e = jnp.sqrt(jnp.sum(emb * emb, axis=-1, keepdims=True) + eps_norm)
    norm_r = jnp.sqrt(jnp.sum(refer * refer, axis=-1, keepdims=True) + eps_norm)
    cosine = jnp.sum(emb * refer, axis=-1, keepdims=True) / (norm_e * norm_r)
    d_embed = (
        loss_scale * (refer / (norm_e * norm_r) - cosine * emb / (norm_e * norm_e))
    ).astype(BF)
    d_feature = dot(d_embed, w_embed[...], 1, 1)
    d_pre = (d_feature * gelu_slope(face_ref[0:8])).astype(BF)
    parts = [
        dot(d_pre, w_feature[256 * g : 256 * g + 256, :], 1, 1) for g in range(GROUPS)
    ]
    d_crop = jnp.concatenate(parts, axis=0).astype(BF)
    last = dot(d_pre, w_feature[GROUPS * 256 : CROP, :], 1, 1).astype(BF)
    index = lax.broadcasted_iota(jnp.int32, (TOK, ROWS), 1)
    token = lax.broadcasted_iota(jnp.int32, (TOK, ROWS), 0)
    tail = lax.broadcasted_iota(jnp.int32, (TOK, 8), 1) + ROWS
    pick = (token_of(rows, cols, tail, 0) == token[:, 0:8]).astype(BF)
    d_latent = dot(pick, last, 1, 0)
    for i in range(4):
        pick = (token_of(rows, cols, index, i) == token).astype(BF)
        piece = dot(d_crop, shifted(CH, 256, CH * i), 1, 1).astype(BF)
        d_latent += dot(pick, piece, 1, 0)
    d_latent = d_latent.astype(BF)
    latent_ref[...] = d_latent
    lane = lax.broadcasted_iota(jnp.int32, (KH, 128), 1)
    for p in range(8):
        part = dot(d_latent, x_ref[:, p * PAIR : p * PAIR + PAIR], 0, 0)
        for u in range(6):
            top = part[0:KH, 128 * (u // 2) : 128 * (u // 2) + 128]
            bottom = part[KH : 2 * KH, 128 * (u // 2) : 128 * (u // 2) + 128]
            if u % 2 == 0:
                unit = jnp.where(lane < 64, top, pltpu.roll(bottom, 64, 1))
            else:
                unit = jnp.where(lane < 64, pltpu.roll(top, 64, 1), bottom)
            j = 2 * p + u // 3
            share(half, unit.astype(BF), keep, give, 4 * (j % 4) + j // 4, u % 3)


def share(half, unit, keep, give, j, u):
    top, bottom = unit[0 : KH // 2], unit[KH // 2 : KH]
    keep[j, u] = jnp.where(half == 0, top, bottom)
    give[j, u] = jnp.where(half == 0, bottom, top)


def main(*args):
    shares = jax.ShapeDtypeStruct((16, 3, KH // 2, 128), BF)
    return pl.pallas_call(
        main_kernel,
        out_shape=(shares, shares, jax.ShapeDtypeStruct((TOK, CH), BF)),
        in_specs=[SMEM] * 4 + vmem(12),
        out_specs=tuple(vmem(3)),
        compiler_params=params(24),
        cost_estimate=cost(3),
        name="main",
    )(*args)


def through_kernel(latent, maps, *refs):
    blocks, (out, cross_ref, stack, slab, sems) = refs[0:8], refs[8:]
    f, c = lax.axis_index("fsdp"), lax.axis_index("dp") & 1
    total = jnp.zeros((CH, 128), F32)
    for p, tiles, beside in side_by_side(f, c, 1, blocks):
        total += beside
        for t in range(3):
            stack[0:CH, pl.ds(pl.multiple_of(p * PAIR + 128 * t, 128), 128)] = tiles[t]
    cross_ref[...] = dot(total.astype(BF), shifted(CH, 128, 64), 1, 1).astype(BF)
    stack[CH : CH + RANK, :] = maps[...]
    widen = shifted(CH, 128, 0).astype(F32) + dot(cross_ref[...], shifted(RANK, 128, CH), 1, 0)
    wide = dot(latent[...], widen.astype(BF), 1, 0).astype(BF)
    copies = []
    for i in range(D // BLOCK):
        slab[i] = dot(wide, stack[:, BLOCK * i : BLOCK * i + BLOCK], 1, 0).astype(BF)
        copy = pltpu.make_async_copy(
            slab.at[i], out.at[:, pl.ds(BLOCK * i, BLOCK)], sems.at[i]
        )
        copy.start()
        copies.append(copy)
    for copy in copies:
        copy.wait()


def through(*args):
    return pl.pallas_call(
        through_kernel,
        out_shape=(
            jax.ShapeDtypeStruct((TOK, D), BF),
            jax.ShapeDtypeStruct((CH, RANK), BF),
        ),
        in_specs=vmem(10),
        out_specs=(pl.BlockSpec(memory_space=pl.ANY), pl.BlockSpec(memory_space=pltpu.VMEM)),
        scratch_shapes=[
            pltpu.VMEM((CH + RANK, D), BF),
            pltpu.VMEM((D // BLOCK, TOK, BLOCK), BF),
            pltpu.SemaphoreType.DMA((D // BLOCK,)),
        ],
        compiler_params=params(16),
        cost_estimate=cost(3),
        name="through",
    )(*args)


def last_kernel(units, cross, own_proj, grad_a, grad_b):
    unit = [units[u] for u in range(4)]

    def rows(right):
        total = jnp.zeros((KH, SHARD), F32)
        for u in range(3):
            r = lax.broadcasted_iota(jnp.int32, (128, SHARD), 0) - 64 * right
            col = lax.broadcasted_iota(jnp.int32, (128, SHARD), 1) - 64 * u
            place_at = ((r == col) & (col >= 0) & (col < 64)).astype(BF)
            total += dot(unit[u], place_at, 1, 0)
        return total

    sums = jnp.concatenate([rows(0), rows(1)], axis=0).astype(BF)
    low = jnp.concatenate(
        [dot(unit[3], shifted(RANK, 128, 64 * h), 1, 1) for h in range(2)], axis=0
    ).astype(BF)
    grad_a[...] = dot(cross[...], sums, 0, 0) / loss_scale
    grad_b[...] = dot(low, own_proj[...], 0, 0) / loss_scale


def last(*args):
    return pl.pallas_call(
        last_kernel,
        out_shape=(
            jax.ShapeDtypeStruct((RANK, SHARD), F32),
            jax.ShapeDtypeStruct((RANK, SHARD), F32),
        ),
        in_specs=vmem(3),
        out_specs=tuple(vmem(2)),
        compiler_params=params(8),
        cost_estimate=cost(1),
        name="last",
    )(*args)


def add(*terms):
    return sum(t.astype(F32) for t in terms).astype(BF)


def fan(value, **axis):
    ((name, _),) = axis.items()
    return [send(value, flip(**{name: k, "c": 1})) for k in (1, 2, 3)]


def parity(f, d):
    return (d ^ (d >> 1) ^ f ^ (f >> 2)) & 1


def exchange(v, groups):
    v = lax.all_to_all(v, AXES, 0, 0, axis_index_groups=groups, tiled=True)
    return jnp.sum(v.astype(F32), axis=0).astype(BF)


def beside(v, low):
    return jnp.concatenate([v, jnp.broadcast_to(low[None], v.shape[:1] + low.shape)], axis=1)


def shift_z(step):
    def move(zl, y, zh, x, c):
        z = (zh * 4 + zl + step) % 8
        return z % 4, y, z // 4, x, c

    return [(i, number(*move(*coords(i)))) for i in range(256)]


def slab_of(value, start, size):
    return lax.dynamic_slice_in_dim(value, start, size, axis=0)


def members(key):
    groups = {}
    for i in range(256):
        groups.setdefault(key(*coords(i)), []).append(i)
    return list(groups.values())


def reduce_all(keep, give, keep_low, give_low, f, half):
    zl, y = f // 4, f % 4
    v = add(keep, send(give, flip(c=1)))
    low = add(keep_low, send(give_low, flip(c=1)))
    v = v.reshape((4, 12) + v.shape[2:])
    part = lambda k: jnp.concatenate([slab_of(v, y ^ k, 1)[0], low])
    v = add(part(0), *[send(part(k), flip(y=k, c=k & 1)) for k in (2, 1, 3)])
    v, low = v[:12].reshape((4, 3) + v.shape[1:]), v[12:]
    v = beside(v, low)
    v = jnp.broadcast_to(v[:, None], (4, 2) + v.shape[1:]).reshape((8,) + v.shape[1:])
    v = exchange(v, members(lambda zl, y, zh, x, c: (y, x, c ^ (zl & 1))))
    other = send(v, flip(c=1))
    v = jnp.concatenate([jnp.where(half == 0, v, other), jnp.where(half == 0, other, v)], axis=1)
    return add(v, *fan(v, x=0))


def local(
    block_in,
    block_out,
    weight,
    adapter_a,
    adapter_b,
    proj,
    w_feature,
    w_embed,
    id_table,
    box_rows,
    box_cols,
    identity,
    face_count,
):
    f, d = lax.axis_index("fsdp"), lax.axis_index("dp")
    proj_t = proj.T

    table = jnp.concatenate([id_table, send(id_table, flip(zl=2, zh=1, c=1))])
    maps, own_proj, faces = front(
        box_rows, box_cols, proj_t, weight, adapter_a.T, adapter_b,
        block_out, w_feature, w_embed,
    )
    maps = after(maps, table)
    tables = fan(table, x=0)
    maps = jnp.concatenate([maps] + fan(maps, zl=0))
    tables = [table] + tables
    blocks = [maps] + fan(maps, y=0)
    tables += [send(part, flip(c=1)) for part in tables]
    blocks += [send(part, flip(c=1)) for part in blocks]
    keep, give, d_latent = main(
        box_rows, box_cols, identity, face_count,
        *tables, faces, w_embed, w_feature, block_in,
    )
    whole_a, keep_low, give_low = low_maps(block_in, d_latent, *blocks)
    total = reduce_all(keep, give, keep_low, give_low, f, parity(f, d))
    grad_in, cross = through(d_latent, whole_a, *blocks)
    grad_a, grad_b = last(total, cross, own_proj)
    return grad_in, grad_a.T, grad_b


def solution(mesh):
    return jax.shard_map(
        local,
        mesh=mesh,
        in_specs=(
            P(("fsdp", "dp"), None),
            P(("fsdp", "dp"), None),
            P("fsdp", None),
            P("fsdp", None),
            P(None, "fsdp"),
            P(),
            P(),
            P(),
            P("dp", None),
            P(("fsdp", "dp"), None),
            P(("fsdp", "dp"), None),
            P(("fsdp", "dp"), None),
            P(("fsdp", "dp")),
        ),
        out_specs=(P(("fsdp", "dp"), None), P("fsdp", None), P(None, "fsdp")),
        check_vma=False,
    )
```

```python
import jax
import jax.numpy as jnp
from jax import lax
from jax.experimental import pallas as pl
from jax.experimental.pallas import tpu as pltpu
from jax.sharding import PartitionSpec as P

D = 3072
CH = 64
RANK = 64
HID = 512
EMB = 512
FACE = 7
MAXF = 6
GW = 16
IDS_DEV = 64
TOK = 256
CROP = 3136
SHARD = 192
PAIR = 2 * SHARD
KH = 32
GROUPS = 12
ROWS = GROUPS * 8
UNITS = 48
BLOCK = 512

loss_scale = 1024.0
eps_norm = 1e-06
BF = jnp.bfloat16
F32 = jnp.float32
AXES = ("fsdp", "dp")


def coords(index):
    f, d = index // 16, index % 16
    return f // 4, f % 4, d // 8, (d // 2) % 4, d % 2


def number(zl, y, zh, x, c):
    return (zl * 4 + y) * 16 + zh * 8 + x * 2 + c


def flip(zl=0, y=0, zh=0, x=0, c=0):
    move = lambda l, b, h, a, e: (l ^ zl, b ^ y, h ^ zh, a ^ x, e ^ c)
    return [(i, number(*move(*coords(i)))) for i in range(256)]


def send(value, perm):
    return lax.ppermute(value, AXES, perm)


def after(value, *others):
    return lax.optimization_barrier((value,) + others)[0]


def dot(a, b, da, db):
    return lax.dot_general(a, b, (((da,), (db,)), ((), ())), preferred_element_type=F32)


def shifted(rows, width, offset):
    r = lax.broadcasted_iota(jnp.int32, (rows, width), 0)
    c = lax.broadcasted_iota(jnp.int32, (rows, width), 1)
    return (c == r + offset).astype(BF)


def params(mib):
    return pltpu.CompilerParams(vmem_limit_bytes=mib << 20)


def cost(us):
    return pl.CostEstimate(flops=us, bytes_accessed=us, transcendentals=0)


def vmem(n):
    return [pl.BlockSpec(memory_space=pltpu.VMEM)] * n


SMEM = pl.BlockSpec(memory_space=pltpu.SMEM)


HBM = pl.BlockSpec(memory_space=pl.ANY)


def corner_of(rows, cols, slot):
    corner = jnp.zeros_like(slot)
    for k in range(MAXF):
        corner = jnp.where(slot == k, rows[0, k] * GW + cols[0, k], corner)
    return corner


def token_of(rows, cols, index, i):
    slot = index & 7
    p = 4 * (index >> 3) + i
    down = (p * 37) >> 8
    token = corner_of(rows, cols, slot) + down * GW + (p - down * FACE)
    return jnp.where((slot < MAXF) & (p < FACE * FACE), token, -1)


def load_all(moves, sems):
    waits, n = [], 0
    for source, target, parts in moves:
        rows = source.shape[0] // parts
        copies = []
        for p in range(parts):
            at = pl.ds(p * rows, rows)
            copies.append(pltpu.make_async_copy(source.at[at], target.at[at], sems.at[n]))
            copies[-1].start()
            n += 1
        waits.append(copies)
    return waits


def arrived(*groups):
    for copies in groups:
        for copy in copies:
            copy.wait()


def front_kernel(
    rows, cols, proj_hbm, weight_hbm, a_hbm, b_hbm, y_hbm, feature_hbm, embed_hbm,
    pay, own_ref, face_ref,
    proj_t, weight, a_ref, b_ref, y_ref, w_feature, w_embed, sems,
):
    f, c = lax.axis_index("fsdp"), lax.axis_index("dp") & 1
    small, heavy, faces, feature_w, embed_w = (slice(0, 3), slice(3, 4), 4, 5, 6)
    copies = load_all(
        (
            (proj_hbm, proj_t, 2),
            (a_hbm, a_ref, 1),
            (b_hbm, b_ref, 1),
            (weight_hbm, weight, 4),
            (y_hbm, y_ref, 4),
            (feature_hbm, w_feature, 7),
            (embed_hbm, w_embed, 2),
        ),
        sems,
    )
    n = ROWS + 8
    index = lax.broadcasted_iota(jnp.int32, (n, TOK), 0)
    token = lax.broadcasted_iota(jnp.int32, (n, TOK), 1)
    picks = [(token_of(rows, cols, index, i) == token).astype(BF) for i in range(4)]
    arrived(*copies[small])
    window = proj_t[:, pl.ds(pl.multiple_of((f >> 1) * PAIR, 128), PAIR)]
    own = dot(window, shifted(SHARD, PAIR, (f & 1) * SHARD), 1, 1).astype(BF)
    own_ref[...] = own
    arrived(*copies[heavy])

    @pl.when(c == 0)
    def _():
        pay[0] = dot(a_ref[...], shifted(SHARD, 256, 0), 1, 0).astype(BF)

    @pl.when(c == 1)
    def _():
        moved = (dot(proj_t[...], weight[...], 1, 1) + own.astype(F32)).astype(BF)
        cross = dot(own, b_ref[...], 1, 1).astype(BF)
        wide = dot(moved, shifted(SHARD, 256, 0), 1, 0)
        pay[0] = (wide + dot(cross, shifted(CH, 256, SHARD), 1, 0)).astype(BF)

    arrived(copies[faces])
    latent = dot(y_ref[...], proj_t[...], 1, 1).astype(BF)
    crops = jnp.zeros((n, 256), F32)
    for i in range(4):
        piece = dot(picks[i], latent, 1, 0).astype(BF)
        crops += dot(piece, shifted(CH, 256, CH * i), 1, 0)
    crops = crops.astype(BF)
    arrived(copies[feature_w])
    pre = dot(crops[ROWS:n, 0:CH], w_feature[GROUPS * 256 : CROP, :], 1, 0)
    for g in range(GROUPS):
        pre += dot(crops[8 * g : 8 * g + 8, :], w_feature[256 * g : 256 * g + 256, :], 1, 0)
    face_ref[0:8] = pre
    feature = jax.nn.gelu(pre).astype(BF)
    arrived(copies[embed_w])
    face_ref[8:16] = dot(feature, w_embed[...], 1, 0)


def front(*args):
    return pl.pallas_call(
        front_kernel,
        out_shape=(
            jax.ShapeDtypeStruct((1, CH, 256), BF),
            jax.ShapeDtypeStruct((CH, SHARD), BF),
            jax.ShapeDtypeStruct((16, EMB), F32),
        ),
        in_specs=[SMEM] * 2 + [HBM] * 7,
        out_specs=tuple(vmem(3)),
        scratch_shapes=[
            pltpu.VMEM((CH, D), BF),
            pltpu.VMEM((SHARD, D), BF),
            pltpu.VMEM((RANK, SHARD), BF),
            pltpu.VMEM((RANK, SHARD), BF),
            pltpu.VMEM((TOK, D), BF),
            pltpu.VMEM((CROP, HID), BF),
            pltpu.VMEM((HID, EMB), BF),
            pltpu.SemaphoreType.DMA((21,)),
        ],
        compiler_params=params(56),
        cost_estimate=cost(4),
        name="front",
    )(*args)


def side_by_side(f, c, kind, maps):
    zl, y = f >> 2, f & 3
    even = (y & 1) == 0
    lane = lax.broadcasted_iota(jnp.int32, (CH, 128), 1)

    def block(k, i):
        crossed = int(k != 0) ^ int(i != 0)
        return jnp.where((c ^ crossed) == kind, maps[k][i], maps[k + 4][i])

    for k in (0, 2):
        for i in range(4):
            a, b = block(k, i), block(k + 1, i)
            left = jnp.where(even, a, b).astype(F32)
            right = jnp.where(even, b, a).astype(F32)
            turned = pltpu.roll(right[:, 0:128], 64, 1)
            tiles = (
                left[:, 0:128],
                jnp.where(lane < 64, left[:, 128:256], turned),
                jnp.where(lane < 64, turned, pltpu.roll(right[:, 128:256], 64, 1)),
            )
            p = (zl ^ i) * 2 + ((y ^ k) >> 1)
            yield p, [t.astype(BF) for t in tiles], left[:, 128:256] + right[:, 128:256]


def low_kernel(x_ref, latent, *refs):
    blocks, (maps, keep, give) = refs[0:8], refs[8:]
    f, c = lax.axis_index("fsdp"), lax.axis_index("dp") & 1
    total = jnp.zeros((TOK, RANK), F32)
    for p, tiles, _ in side_by_side(f, c, 0, blocks):
        for t in range(3):
            spot = pl.ds(pl.multiple_of(p * PAIR + 128 * t, 128), 128)
            maps[:, spot] = tiles[t]
        spot = pl.ds(pl.multiple_of(p * PAIR, 128), PAIR)
        total += dot(x_ref[:, spot], maps[:, spot], 1, 1)
    part = dot(latent[...], dot(total.astype(BF), shifted(RANK, 128, 0), 1, 0).astype(BF), 1, 0)
    lane = lax.broadcasted_iota(jnp.int32, (KH, 128), 1)
    unit = jnp.where(lane < 64, part[0:KH], pltpu.roll(part[KH : 2 * KH], 64, 1)).astype(BF)
    top, bottom = unit[0 : KH // 2], unit[KH // 2 : KH]
    half = parity(f, lax.axis_index("dp"))
    keep[0] = jnp.where(half == 0, top, bottom)
    give[0] = jnp.where(half == 0, bottom, top)


def low_maps(*args):
    share = jax.ShapeDtypeStruct((1, KH // 2, 128), BF)
    return pl.pallas_call(
        low_kernel,
        out_shape=(jax.ShapeDtypeStruct((RANK, D), BF), share, share),
        in_specs=vmem(10),
        out_specs=tuple(vmem(3)),
        compiler_params=params(16),
        cost_estimate=cost(2),
        name="low",
    )(*args)


def gelu_slope(preact):
    return jax.jvp(jax.nn.gelu, (preact,), (jnp.ones_like(preact),))[1]


def main_kernel(
    rows, cols, ident, count, *refs,
):
    near, far = refs[0:4], refs[4:8]
    face_ref, w_embed, w_feature, x_ref, keep, give, latent_ref = refs[8:]
    d = lax.axis_index("dp")
    half = parity(lax.axis_index("fsdp"), d)
    slot = lax.broadcasted_iota(jnp.int32, (8, 16 * MAXF), 0)
    lane = lax.broadcasted_iota(jnp.int32, (8, 16 * MAXF), 1)
    live = jnp.zeros(slot.shape, jnp.bool_)
    chunks = []
    for k_slot in range(MAXF):
        who = ident[0, k_slot]
        apart = (who >> 6) ^ d
        dz, dx = apart >> 3, (apart >> 1) & 3
        crossed = dz ^ jnp.where(dx == 0, 0, 1)
        here = ((apart ^ crossed) & 1) == 0
        spot = dz * IDS_DEV + (who & 63)
        at = pl.ds(pl.multiple_of((spot >> 4) * 16, 16), 16)
        found = jnp.zeros((16, EMB), BF)
        for k in range(4):
            found = jnp.where(dx == k, jnp.where(here, near[k][at, :], far[k][at, :]), found)
        hit = (slot == k_slot) & (lane == 16 * k_slot + (spot & 15))
        live = live | (hit & (k_slot < count[0]))
        chunks.append(found)
    refer = dot(live.astype(BF), jnp.concatenate(chunks, axis=0), 1, 0)
    emb = face_ref[8:16]
    norm_e = jnp.sqrt(jnp.sum(emb * emb, axis=-1, keepdims=True) + eps_norm)
    norm_r = jnp.sqrt(jnp.sum(refer * refer, axis=-1, keepdims=True) + eps_norm)
    cosine = jnp.sum(emb * refer, axis=-1, keepdims=True) / (norm_e * norm_r)
    d_embed = (
        loss_scale * (refer / (norm_e * norm_r) - cosine * emb / (norm_e * norm_e))
    ).astype(BF)
    d_feature = dot(d_embed, w_embed[...], 1, 1)
    d_pre = (d_feature * face_ref[0:8]).astype(BF)
    parts = [
        dot(d_pre, w_feature[256 * g : 256 * g + 256, :], 1, 1) for g in range(GROUPS)
    ]
    d_crop = jnp.concatenate(parts, axis=0).astype(BF)
    last = dot(d_pre, w_feature[GROUPS * 256 : CROP, :], 1, 1).astype(BF)
    index = lax.broadcasted_iota(jnp.int32, (ROWS, TOK), 0)
    token = lax.broadcasted_iota(jnp.int32, (ROWS, TOK), 1)
    tail = index[0:8] + ROWS
    pick = (token_of(rows, cols, tail, 0) == token[0:8]).astype(BF)
    d_latent = dot(last, pick, 0, 0)
    for i in range(4):
        pick = (token_of(rows, cols, index, i) == token).astype(BF)
        piece = dot(shifted(CH, 256, CH * i), d_crop, 1, 1).astype(BF)
        d_latent += dot(piece, pick, 1, 0)
    d_latent = d_latent.astype(BF)
    latent_ref[...] = d_latent
    lane = lax.broadcasted_iota(jnp.int32, (KH, 128), 1)
    for p in range(8):
        part = dot(d_latent, x_ref[:, p * PAIR : p * PAIR + PAIR], 1, 0)
        for u in range(6):
            top = part[0:KH, 128 * (u // 2) : 128 * (u // 2) + 128]
            bottom = part[KH : 2 * KH, 128 * (u // 2) : 128 * (u // 2) + 128]
            if u % 2 == 0:
                unit = jnp.where(lane < 64, top, pltpu.roll(bottom, 64, 1))
            else:
                unit = jnp.where(lane < 64, pltpu.roll(top, 64, 1), bottom)
            j = 2 * p + u // 3
            share(half, unit.astype(BF), keep, give, 4 * (j % 4) + j // 4, u % 3)


def share(half, unit, keep, give, j, u):
    top, bottom = unit[0 : KH // 2], unit[KH // 2 : KH]
    keep[j, u] = jnp.where(half == 0, top, bottom)
    give[j, u] = jnp.where(half == 0, bottom, top)


def main(*args):
    shares = jax.ShapeDtypeStruct((16, 3, KH // 2, 128), BF)
    return pl.pallas_call(
        main_kernel,
        out_shape=(shares, shares, jax.ShapeDtypeStruct((CH, TOK), BF)),
        in_specs=[SMEM] * 4 + vmem(12),
        out_specs=tuple(vmem(3)),
        compiler_params=params(24),
        cost_estimate=cost(3),
        name="main",
    )(*args)


def through_kernel(latent, maps, *refs):
    blocks, (out, cross_ref, stack, slab, sems) = refs[0:8], refs[8:]
    f, c = lax.axis_index("fsdp"), lax.axis_index("dp") & 1
    total = jnp.zeros((CH, 128), F32)
    for p, tiles, beside in side_by_side(f, c, 1, blocks):
        total += beside
        for t in range(3):
            stack[0:CH, pl.ds(pl.multiple_of(p * PAIR + 128 * t, 128), 128)] = tiles[t]
    cross_ref[...] = dot(total.astype(BF), shifted(CH, 128, 64), 1, 1).astype(BF)
    stack[CH : CH + RANK, :] = maps[...]
    widen = shifted(CH, 128, 0).astype(F32) + dot(cross_ref[...], shifted(RANK, 128, CH), 1, 0)
    wide = dot(latent[...], widen.astype(BF), 0, 0).astype(BF)
    copies = []
    for i in range(D // BLOCK):
        slab[i] = dot(wide, stack[:, BLOCK * i : BLOCK * i + BLOCK], 1, 0).astype(BF)
        copy = pltpu.make_async_copy(
            slab.at[i], out.at[:, pl.ds(BLOCK * i, BLOCK)], sems.at[i]
        )
        copy.start()
        copies.append(copy)
    for copy in copies:
        copy.wait()


def through(*args):
    return pl.pallas_call(
        through_kernel,
        out_shape=(
            jax.ShapeDtypeStruct((TOK, D), BF),
            jax.ShapeDtypeStruct((CH, RANK), BF),
        ),
        in_specs=vmem(10),
        out_specs=(pl.BlockSpec(memory_space=pl.ANY), pl.BlockSpec(memory_space=pltpu.VMEM)),
        scratch_shapes=[
            pltpu.VMEM((CH + RANK, D), BF),
            pltpu.VMEM((D // BLOCK, TOK, BLOCK), BF),
            pltpu.SemaphoreType.DMA((D // BLOCK,)),
        ],
        compiler_params=params(16),
        cost_estimate=cost(3),
        name="through",
    )(*args)


def last_kernel(units, cross, own_proj, grad_a, grad_b):
    unit = [units[u] for u in range(4)]

    def rows(right):
        total = jnp.zeros((KH, SHARD), F32)
        for u in range(3):
            r = lax.broadcasted_iota(jnp.int32, (128, SHARD), 0) - 64 * right
            col = lax.broadcasted_iota(jnp.int32, (128, SHARD), 1) - 64 * u
            place_at = ((r == col) & (col >= 0) & (col < 64)).astype(BF)
            total += dot(unit[u], place_at, 1, 0)
        return total

    sums = jnp.concatenate([rows(0), rows(1)], axis=0).astype(BF)
    low = jnp.concatenate(
        [dot(unit[3], shifted(RANK, 128, 64 * h), 1, 1) for h in range(2)], axis=0
    ).astype(BF)
    grad_a[...] = dot(cross[...], sums, 0, 0) / loss_scale
    grad_b[...] = dot(low, own_proj[...], 0, 0) / loss_scale


def last(*args):
    return pl.pallas_call(
        last_kernel,
        out_shape=(
            jax.ShapeDtypeStruct((RANK, SHARD), F32),
            jax.ShapeDtypeStruct((RANK, SHARD), F32),
        ),
        in_specs=vmem(3),
        out_specs=tuple(vmem(2)),
        compiler_params=params(8),
        cost_estimate=cost(1),
        name="last",
    )(*args)


def add(*terms):
    return sum(t.astype(F32) for t in terms).astype(BF)


def fan(value, order, **axis):
    ((name, _),) = axis.items()
    parts = {k: send(value, flip(**{name: k, "c": 1})) for k in order}
    return [parts[k] for k in (1, 2, 3)]


def parity(f, d):
    return (d ^ (d >> 1) ^ f ^ (f >> 2)) & 1


def exchange(v, groups):
    v = lax.all_to_all(v, AXES, 0, 0, axis_index_groups=groups, tiled=True)
    return jnp.sum(v.astype(F32), axis=0).astype(BF)


def beside(v, low):
    return jnp.concatenate([v, jnp.broadcast_to(low[None], v.shape[:1] + low.shape)], axis=1)


def shift_z(step):
    def move(zl, y, zh, x, c):
        z = (zh * 4 + zl + step) % 8
        return z % 4, y, z // 4, x, c

    return [(i, number(*move(*coords(i)))) for i in range(256)]


def slab_of(value, start, size):
    return lax.dynamic_slice_in_dim(value, start, size, axis=0)


def members(key):
    groups = {}
    for i in range(256):
        groups.setdefault(key(*coords(i)), []).append(i)
    return list(groups.values())


def reduce_all(keep, give, keep_low, give_low, f, half):
    zl, y = f // 4, f % 4
    v = add(keep, send(give, flip(c=1)))
    low = add(keep_low, send(give_low, flip(c=1)))
    v = v.reshape((4, 12) + v.shape[2:])
    part = lambda k: jnp.concatenate([slab_of(v, y ^ k, 1)[0], low])
    v = add(part(0), *[send(part(k), flip(y=k, c=k & 1)) for k in (2, 1, 3)])
    v, low = v[:12].reshape((4, 3) + v.shape[1:]), v[12:]
    v = beside(v, low)
    v = jnp.broadcast_to(v[:, None], (4, 2) + v.shape[1:]).reshape((8,) + v.shape[1:])
    v = exchange(v, members(lambda zl, y, zh, x, c: (y, x, c ^ (zl & 1))))
    other = send(v, flip(c=1))
    v = jnp.concatenate([jnp.where(half == 0, v, other), jnp.where(half == 0, other, v)], axis=1)
    return add(v, *fan(v, (1, 2, 3), x=0))


def local(
    block_in,
    block_out,
    weight,
    adapter_a,
    adapter_b,
    proj,
    w_feature,
    w_embed,
    id_table,
    box_rows,
    box_cols,
    identity,
    face_count,
):
    f, d = lax.axis_index("fsdp"), lax.axis_index("dp")
    proj_t = proj.T

    table = jnp.concatenate([id_table, send(id_table, flip(zl=2, zh=1, c=1))])
    maps, own_proj, faces = front(
        box_rows, box_cols, proj_t, weight, adapter_a.T, adapter_b,
        block_out, w_feature, w_embed,
    )
    maps = after(maps, table)
    tables = fan(table, (1, 2, 3), x=0)
    maps = jnp.concatenate([maps] + fan(maps, (1, 2, 3), zl=0))
    tables = [table] + tables
    blocks = [maps] + fan(maps, (1, 2, 3), y=0)
    faces = after(faces, maps)
    upper = lax.broadcasted_iota(jnp.int32, faces.shape, 0) < 8
    faces = jnp.where(upper, gelu_slope(faces), faces)
    tables += [send(part, flip(c=1)) for part in tables]
    blocks += [send(part, flip(c=1)) for part in blocks]
    keep, give, d_latent = main(
        box_rows, box_cols, identity, face_count,
        *tables, faces, w_embed, w_feature, block_in,
    )
    whole_a, keep_low, give_low = low_maps(block_in, d_latent, *blocks)
    total = reduce_all(keep, give, keep_low, give_low, f, parity(f, d))
    grad_in, cross = through(d_latent, whole_a, *blocks)
    grad_a, grad_b = last(total, cross, own_proj)
    return grad_in, grad_a.T, grad_b


def solution(mesh):
    return jax.shard_map(
        local,
        mesh=mesh,
        in_specs=(
            P(("fsdp", "dp"), None),
            P(("fsdp", "dp"), None),
            P("fsdp", None),
            P("fsdp", None),
            P(None, "fsdp"),
            P(),
            P(),
            P(),
            P("dp", None),
            P(("fsdp", "dp"), None),
            P(("fsdp", "dp"), None),
            P(("fsdp", "dp"), None),
            P(("fsdp", "dp")),
        ),
        out_specs=(P(("fsdp", "dp"), None), P("fsdp", None), P(None, "fsdp")),
        check_vma=False,
    )
```

```python
import jax
import jax.numpy as jnp
from jax import lax
from jax.experimental import pallas as pl
from jax.experimental.pallas import tpu as pltpu
from jax.sharding import PartitionSpec as P

D = 3072
CH = 64
RANK = 64
HID = 512
EMB = 512
FACE = 7
MAXF = 6
GW = 16
IDS_DEV = 64
TOK = 256
CROP = 3136
SHARD = 192
PAIR = 2 * SHARD
KH = 32
GROUPS = 12
ROWS = GROUPS * 8
UNITS = 48
BLOCK = 512

loss_scale = 1024.0
eps_norm = 1e-06
BF = jnp.bfloat16
F32 = jnp.float32
AXES = ("fsdp", "dp")


def coords(index):
    f, d = index // 16, index % 16
    return f // 4, f % 4, d // 8, (d // 2) % 4, d % 2


def number(zl, y, zh, x, c):
    return (zl * 4 + y) * 16 + zh * 8 + x * 2 + c


def flip(zl=0, y=0, zh=0, x=0, c=0):
    move = lambda l, b, h, a, e: (l ^ zl, b ^ y, h ^ zh, a ^ x, e ^ c)
    return [(i, number(*move(*coords(i)))) for i in range(256)]


def send(value, perm):
    return lax.ppermute(value, AXES, perm)


def after(value, *others):
    return lax.optimization_barrier((value,) + others)[0]


def dot(a, b, da, db):
    return lax.dot_general(a, b, (((da,), (db,)), ((), ())), preferred_element_type=F32)


def shifted(rows, width, offset):
    r = lax.broadcasted_iota(jnp.int32, (rows, width), 0)
    c = lax.broadcasted_iota(jnp.int32, (rows, width), 1)
    return (c == r + offset).astype(BF)


def params(mib):
    return pltpu.CompilerParams(vmem_limit_bytes=mib << 20)


def cost(us):
    return pl.CostEstimate(flops=us, bytes_accessed=us, transcendentals=0)


def vmem(n):
    return [pl.BlockSpec(memory_space=pltpu.VMEM)] * n


SMEM = pl.BlockSpec(memory_space=pltpu.SMEM)


HBM = pl.BlockSpec(memory_space=pl.ANY)


def corner_of(rows, cols, slot):
    corner = jnp.zeros_like(slot)
    for k in range(MAXF):
        corner = jnp.where(slot == k, rows[0, k] * GW + cols[0, k], corner)
    return corner


def token_of(rows, cols, index, i):
    slot = index & 7
    p = 4 * (index >> 3) + i
    down = (p * 37) >> 8
    token = corner_of(rows, cols, slot) + down * GW + (p - down * FACE)
    return jnp.where((slot < MAXF) & (p < FACE * FACE), token, -1)


def load_all(moves, sems):
    waits, n = [], 0
    for source, target, parts in moves:
        rows = source.shape[0] // parts
        copies = []
        for p in range(parts):
            at = pl.ds(p * rows, rows)
            copies.append(pltpu.make_async_copy(source.at[at], target.at[at], sems.at[n]))
            copies[-1].start()
            n += 1
        waits.append(copies)
    return waits


def arrived(*groups):
    for copies in groups:
        for copy in copies:
            copy.wait()


def front_kernel(
    rows, cols, proj_hbm, weight_hbm, a_hbm, b_hbm, y_hbm, feature_hbm, embed_hbm,
    pay, own_ref, face_ref,
    proj_t, weight, a_ref, b_ref, y_ref, w_feature, w_embed, sems,
):
    f, c = lax.axis_index("fsdp"), lax.axis_index("dp") & 1
    small, heavy, faces, feature_w, embed_w = (slice(0, 3), slice(3, 4), 4, 5, 6)
    copies = load_all(
        (
            (proj_hbm, proj_t, 2),
            (a_hbm, a_ref, 1),
            (b_hbm, b_ref, 1),
            (weight_hbm, weight, 4),
            (y_hbm, y_ref, 4),
            (feature_hbm, w_feature, 7),
            (embed_hbm, w_embed, 2),
        ),
        sems,
    )
    n = ROWS + 8
    index = lax.broadcasted_iota(jnp.int32, (n, TOK), 0)
    token = lax.broadcasted_iota(jnp.int32, (n, TOK), 1)
    picks = [(token_of(rows, cols, index, i) == token).astype(BF) for i in range(4)]
    arrived(*copies[small])
    window = proj_t[:, pl.ds(pl.multiple_of((f >> 1) * PAIR, 128), PAIR)]
    own = dot(window, shifted(SHARD, PAIR, (f & 1) * SHARD), 1, 1).astype(BF)
    own_ref[...] = own
    arrived(*copies[heavy])

    @pl.when(c == 0)
    def _():
        pay[0] = dot(a_ref[...], shifted(SHARD, 256, 0), 1, 0).astype(BF)

    @pl.when(c == 1)
    def _():
        moved = (dot(proj_t[...], weight[...], 1, 1) + own.astype(F32)).astype(BF)
        cross = dot(own, b_ref[...], 1, 1).astype(BF)
        wide = dot(moved, shifted(SHARD, 256, 0), 1, 0)
        pay[0] = (wide + dot(cross, shifted(CH, 256, SHARD), 1, 0)).astype(BF)

    arrived(copies[faces])
    latent = dot(y_ref[...], proj_t[...], 1, 1).astype(BF)
    crops = jnp.zeros((n, 256), F32)
    for i in range(4):
        piece = dot(picks[i], latent, 1, 0).astype(BF)
        crops += dot(piece, shifted(CH, 256, CH * i), 1, 0)
    crops = crops.astype(BF)
    arrived(copies[feature_w])
    pre = dot(crops[ROWS:n, 0:CH], w_feature[GROUPS * 256 : CROP, :], 1, 0)
    for g in range(GROUPS):
        pre += dot(crops[8 * g : 8 * g + 8, :], w_feature[256 * g : 256 * g + 256, :], 1, 0)
    face_ref[0:8] = pre
    feature = jax.nn.gelu(pre).astype(BF)
    arrived(copies[embed_w])
    face_ref[8:16] = dot(feature, w_embed[...], 1, 0)


def front(*args):
    return pl.pallas_call(
        front_kernel,
        out_shape=(
            jax.ShapeDtypeStruct((1, CH, 256), BF),
            jax.ShapeDtypeStruct((CH, SHARD), BF),
            jax.ShapeDtypeStruct((16, EMB), F32),
        ),
        in_specs=[SMEM] * 2 + [HBM] * 7,
        out_specs=tuple(vmem(3)),
        scratch_shapes=[
            pltpu.VMEM((CH, D), BF),
            pltpu.VMEM((SHARD, D), BF),
            pltpu.VMEM((RANK, SHARD), BF),
            pltpu.VMEM((RANK, SHARD), BF),
            pltpu.VMEM((TOK, D), BF),
            pltpu.VMEM((CROP, HID), BF),
            pltpu.VMEM((HID, EMB), BF),
            pltpu.SemaphoreType.DMA((21,)),
        ],
        compiler_params=params(56),
        cost_estimate=cost(4),
        name="front",
    )(*args)


def side_by_side(f, c, kind, maps):
    zl, y = f >> 2, f & 3
    even = (y & 1) == 0
    lane = lax.broadcasted_iota(jnp.int32, (CH, 128), 1)

    def block(k, i):
        crossed = int(k != 0) ^ int(i != 0)
        return jnp.where((c ^ crossed) == kind, maps[k][i], maps[k + 4][i])

    for k in (0, 2):
        for i in range(4):
            a, b = block(k, i), block(k + 1, i)
            left = jnp.where(even, a, b).astype(F32)
            right = jnp.where(even, b, a).astype(F32)
            turned = pltpu.roll(right[:, 0:128], 64, 1)
            tiles = (
                left[:, 0:128],
                jnp.where(lane < 64, left[:, 128:256], turned),
                jnp.where(lane < 64, turned, pltpu.roll(right[:, 128:256], 64, 1)),
            )
            p = (zl ^ i) * 2 + ((y ^ k) >> 1)
            yield p, [t.astype(BF) for t in tiles], left[:, 128:256] + right[:, 128:256]


def gelu_slope(preact):
    return jax.jvp(jax.nn.gelu, (preact,), (jnp.ones_like(preact),))[1]


def main_kernel(
    rows, cols, ident, count, *refs,
):
    near, far, blocks = refs[0:4], refs[4:8], refs[8:16]
    face_ref, w_embed, w_feature, x_ref, keep, give, latent_ref, maps = refs[16:]
    d = lax.axis_index("dp")
    f, c = lax.axis_index("fsdp"), d & 1
    half = parity(f, d)
    low = jnp.zeros((TOK, RANK), F32)
    for p, tiles, _ in side_by_side(f, c, 0, blocks):
        for t in range(3):
            spot = pl.ds(pl.multiple_of(p * PAIR + 128 * t, 128), 128)
            maps[:, spot] = tiles[t]
        spot = pl.ds(pl.multiple_of(p * PAIR, 128), PAIR)
        low += dot(x_ref[:, spot], maps[:, spot], 1, 1)
    low = dot(low.astype(BF), shifted(RANK, 128, 0), 1, 0).astype(BF)
    slot = lax.broadcasted_iota(jnp.int32, (8, 16 * MAXF), 0)
    lane = lax.broadcasted_iota(jnp.int32, (8, 16 * MAXF), 1)
    live = jnp.zeros(slot.shape, jnp.bool_)
    chunks = []
    for k_slot in range(MAXF):
        who = ident[0, k_slot]
        apart = (who >> 6) ^ d
        dz, dx = apart >> 3, (apart >> 1) & 3
        crossed = dz ^ jnp.where(dx == 0, 0, 1)
        here = ((apart ^ crossed) & 1) == 0
        spot = dz * IDS_DEV + (who & 63)
        at = pl.ds(pl.multiple_of((spot >> 4) * 16, 16), 16)
        found = jnp.zeros((16, EMB), BF)
        for k in range(4):
            found = jnp.where(dx == k, jnp.where(here, near[k][at, :], far[k][at, :]), found)
        hit = (slot == k_slot) & (lane == 16 * k_slot + (spot & 15))
        live = live | (hit & (k_slot < count[0]))
        chunks.append(found)
    refer = dot(live.astype(BF), jnp.concatenate(chunks, axis=0), 1, 0)
    emb = face_ref[8:16]
    norm_e = jnp.sqrt(jnp.sum(emb * emb, axis=-1, keepdims=True) + eps_norm)
    norm_r = jnp.sqrt(jnp.sum(refer * refer, axis=-1, keepdims=True) + eps_norm)
    cosine = jnp.sum(emb * refer, axis=-1, keepdims=True) / (norm_e * norm_r)
    d_embed = (
        loss_scale * (refer / (norm_e * norm_r) - cosine * emb / (norm_e * norm_e))
    ).astype(BF)
    d_feature = dot(d_embed, w_embed[...], 1, 1)
    d_pre = (d_feature * face_ref[0:8]).astype(BF)
    parts = [
        dot(d_pre, w_feature[256 * g : 256 * g + 256, :], 1, 1) for g in range(GROUPS)
    ]
    d_crop = jnp.concatenate(parts, axis=0).astype(BF)
    last = dot(d_pre, w_feature[GROUPS * 256 : CROP, :], 1, 1).astype(BF)
    index = lax.broadcasted_iota(jnp.int32, (ROWS, TOK), 0)
    token = lax.broadcasted_iota(jnp.int32, (ROWS, TOK), 1)
    tail = index[0:8] + ROWS
    pick = (token_of(rows, cols, tail, 0) == token[0:8]).astype(BF)
    d_latent = dot(last, pick, 0, 0)
    for i in range(4):
        pick = (token_of(rows, cols, index, i) == token).astype(BF)
        piece = dot(shifted(CH, 256, CH * i), d_crop, 1, 1).astype(BF)
        d_latent += dot(piece, pick, 1, 0)
    d_latent = d_latent.astype(BF)
    latent_ref[...] = d_latent
    lane = lax.broadcasted_iota(jnp.int32, (KH, 128), 1)
    part = dot(d_latent, low, 1, 0)
    unit = jnp.where(lane < 64, part[0:KH], pltpu.roll(part[KH : 2 * KH], 64, 1))
    for u in range(3):
        share(half, unit.astype(BF), keep, give, 16, u)
    for p in range(8):
        part = dot(d_latent, x_ref[:, p * PAIR : p * PAIR + PAIR], 1, 0)
        for u in range(6):
            top = part[0:KH, 128 * (u // 2) : 128 * (u // 2) + 128]
            bottom = part[KH : 2 * KH, 128 * (u // 2) : 128 * (u // 2) + 128]
            if u % 2 == 0:
                unit = jnp.where(lane < 64, top, pltpu.roll(bottom, 64, 1))
            else:
                unit = jnp.where(lane < 64, pltpu.roll(top, 64, 1), bottom)
            j = 2 * p + u // 3
            share(half, unit.astype(BF), keep, give, 4 * (j % 4) + j // 4, u % 3)


def share(half, unit, keep, give, j, u):
    top, bottom = unit[0 : KH // 2], unit[KH // 2 : KH]
    keep[j, u] = jnp.where(half == 0, top, bottom)
    give[j, u] = jnp.where(half == 0, bottom, top)


def main(*args):
    shares = jax.ShapeDtypeStruct((17, 3, KH // 2, 128), BF)
    return pl.pallas_call(
        main_kernel,
        out_shape=(
            shares,
            shares,
            jax.ShapeDtypeStruct((CH, TOK), BF),
            jax.ShapeDtypeStruct((RANK, D), BF),
        ),
        in_specs=[SMEM] * 4 + vmem(20),
        out_specs=tuple(vmem(4)),
        compiler_params=params(24),
        cost_estimate=cost(3),
        name="main",
    )(*args)


def through_kernel(latent, maps, *refs):
    blocks, (out, cross_ref, stack, slab, sems) = refs[0:8], refs[8:]
    f, c = lax.axis_index("fsdp"), lax.axis_index("dp") & 1
    total = jnp.zeros((CH, 128), F32)
    for p, tiles, beside in side_by_side(f, c, 1, blocks):
        total += beside
        for t in range(3):
            stack[0:CH, pl.ds(pl.multiple_of(p * PAIR + 128 * t, 128), 128)] = tiles[t]
    cross_ref[...] = dot(total.astype(BF), shifted(CH, 128, 64), 1, 1).astype(BF)
    stack[CH : CH + RANK, :] = maps[...]
    widen = shifted(CH, 128, 0).astype(F32) + dot(cross_ref[...], shifted(RANK, 128, CH), 1, 0)
    wide = dot(latent[...], widen.astype(BF), 0, 0).astype(BF)
    copies = []
    for i in range(D // BLOCK):
        slab[i] = dot(wide, stack[:, BLOCK * i : BLOCK * i + BLOCK], 1, 0).astype(BF)
        copy = pltpu.make_async_copy(
            slab.at[i], out.at[:, pl.ds(BLOCK * i, BLOCK)], sems.at[i]
        )
        copy.start()
        copies.append(copy)
    for copy in copies:
        copy.wait()


def through(*args):
    return pl.pallas_call(
        through_kernel,
        out_shape=(
            jax.ShapeDtypeStruct((TOK, D), BF),
            jax.ShapeDtypeStruct((CH, RANK), BF),
        ),
        in_specs=vmem(10),
        out_specs=(pl.BlockSpec(memory_space=pl.ANY), pl.BlockSpec(memory_space=pltpu.VMEM)),
        scratch_shapes=[
            pltpu.VMEM((CH + RANK, D), BF),
            pltpu.VMEM((D // BLOCK, TOK, BLOCK), BF),
            pltpu.SemaphoreType.DMA((D // BLOCK,)),
        ],
        compiler_params=params(16),
        cost_estimate=cost(3),
        name="through",
    )(*args)


def last_kernel(units, cross, own_proj, grad_a, grad_b):
    unit = [units[u] for u in range(4)]

    def rows(right):
        total = jnp.zeros((KH, SHARD), F32)
        for u in range(3):
            r = lax.broadcasted_iota(jnp.int32, (128, SHARD), 0) - 64 * right
            col = lax.broadcasted_iota(jnp.int32, (128, SHARD), 1) - 64 * u
            place_at = ((r == col) & (col >= 0) & (col < 64)).astype(BF)
            total += dot(unit[u], place_at, 1, 0)
        return total

    sums = jnp.concatenate([rows(0), rows(1)], axis=0).astype(BF)
    low = jnp.concatenate(
        [dot(unit[3], shifted(RANK, 128, 64 * h), 1, 1) for h in range(2)], axis=0
    ).astype(BF)
    grad_a[...] = dot(cross[...], sums, 0, 0) / loss_scale
    grad_b[...] = dot(low, own_proj[...], 0, 0) / loss_scale


def last(*args):
    return pl.pallas_call(
        last_kernel,
        out_shape=(
            jax.ShapeDtypeStruct((RANK, SHARD), F32),
            jax.ShapeDtypeStruct((RANK, SHARD), F32),
        ),
        in_specs=vmem(3),
        out_specs=tuple(vmem(2)),
        compiler_params=params(8),
        cost_estimate=cost(1),
        name="last",
    )(*args)


def add(*terms):
    return sum(t.astype(F32) for t in terms).astype(BF)


def fan(value, order, **axis):
    ((name, _),) = axis.items()
    parts = {k: send(value, flip(**{name: k, "c": 1})) for k in order}
    return [parts[k] for k in (1, 2, 3)]


def parity(f, d):
    return (d ^ (d >> 1) ^ f ^ (f >> 2)) & 1


def exchange(v, groups):
    v = lax.all_to_all(v, AXES, 0, 0, axis_index_groups=groups, tiled=True)
    return jnp.sum(v.astype(F32), axis=0).astype(BF)


def beside(v, low):
    return jnp.concatenate([v, jnp.broadcast_to(low[None], v.shape[:1] + low.shape)], axis=1)


def shift_z(step):
    def move(zl, y, zh, x, c):
        z = (zh * 4 + zl + step) % 8
        return z % 4, y, z // 4, x, c

    return [(i, number(*move(*coords(i)))) for i in range(256)]


def slab_of(value, start, size):
    return lax.dynamic_slice_in_dim(value, start, size, axis=0)


def members(key):
    groups = {}
    for i in range(256):
        groups.setdefault(key(*coords(i)), []).append(i)
    return list(groups.values())


def reduce_all(keep, give, f, half):
    zl, y = f // 4, f % 4
    v = add(keep, send(give, flip(c=1)))
    v, low = v[:16], v[16, :1]
    v = v.reshape((4, 12) + v.shape[2:])
    part = lambda k: jnp.concatenate([slab_of(v, y ^ k, 1)[0], low])
    v = add(part(0), *[send(part(k), flip(y=k, c=k & 1)) for k in (3, 1, 2)])
    v, low = v[:12].reshape((4, 3) + v.shape[1:]), v[12:]
    v = beside(v, low)
    v = jnp.broadcast_to(v[:, None], (4, 2) + v.shape[1:]).reshape((8,) + v.shape[1:])
    v = exchange(v, members(lambda zl, y, zh, x, c: (y, x, c ^ (zl & 1))))
    other = send(v, flip(c=1))
    v = jnp.concatenate([jnp.where(half == 0, v, other), jnp.where(half == 0, other, v)], axis=1)
    return add(v, *fan(v, (1, 2, 3), x=0))


def local(
    block_in,
    block_out,
    weight,
    adapter_a,
    adapter_b,
    proj,
    w_feature,
    w_embed,
    id_table,
    box_rows,
    box_cols,
    identity,
    face_count,
):
    f, d = lax.axis_index("fsdp"), lax.axis_index("dp")
    proj_t = proj.T

    table = jnp.concatenate([id_table, send(id_table, flip(zl=2, zh=1, c=1))])
    maps, own_proj, faces = front(
        box_rows, box_cols, proj_t, weight, adapter_a.T, adapter_b,
        block_out, w_feature, w_embed,
    )
    maps = after(maps, table)
    tables = fan(table, (1, 2, 3), x=0)
    maps = jnp.concatenate([maps] + fan(maps, (1, 2, 3), zl=0))
    tables = [table] + tables
    blocks = [maps] + fan(maps, (1, 2, 3), y=0)
    faces = after(faces, maps)
    upper = lax.broadcasted_iota(jnp.int32, faces.shape, 0) < 8
    faces = jnp.where(upper, gelu_slope(faces), faces)
    blocks = [maps] + [after(part, faces) for part in blocks[1:]]
    tables += [send(part, flip(c=1)) for part in tables]
    blocks += [send(part, flip(c=1)) for part in blocks]
    keep, give, d_latent, whole_a = main(
        box_rows, box_cols, identity, face_count,
        *tables, *blocks, faces, w_embed, w_feature, block_in,
    )
    total = reduce_all(keep, give, f, parity(f, d))
    grad_in, cross = through(d_latent, whole_a, *blocks)
    grad_a, grad_b = last(total, cross, own_proj)
    return grad_in, grad_a.T, grad_b


def solution(mesh):
    return jax.shard_map(
        local,
        mesh=mesh,
        in_specs=(
            P(("fsdp", "dp"), None),
            P(("fsdp", "dp"), None),
            P("fsdp", None),
            P("fsdp", None),
            P(None, "fsdp"),
            P(),
            P(),
            P(),
            P("dp", None),
            P(("fsdp", "dp"), None),
            P(("fsdp", "dp"), None),
            P(("fsdp", "dp"), None),
            P(("fsdp", "dp")),
        ),
        out_specs=(P(("fsdp", "dp"), None), P("fsdp", None), P(None, "fsdp")),
        check_vma=False,
    )
```
